256 devices in a mesh: rep: 8 (over z_hi, x), fsdp: 32 (over y, z_lo, core).
Axes of the slice: x: 4, y: 4, z: 8 (z_hi: 2, z_lo: 4; z = z_hi * 4 + z_lo), core: 2. Of those that a mesh axis runs over, the one named last changes fastest.
Arguments:
- images: bfloat16 [256, 16, 32, 320], P(('rep', 'fsdp')), may hold values from -6 to 6
- w_down: bfloat16 [2880, 320], P('fsdp'), may hold values from -0.109375 to 0.109375
- w_conv: bfloat16 [2880, 640], P('fsdp'), may hold values from -0.109375 to 0.109375
- w_skip: bfloat16 [320, 640], P('fsdp'), may hold values from -0.3125 to 0.3125
- act_grad: bfloat16 [256, 8, 16, 640], P(('rep', 'fsdp')), may hold values from -6 to 6
- short_grad: bfloat16 [256, 8, 16, 640], P(('rep', 'fsdp')), may hold values from -6 to 6
Outputs:
- activated: bfloat16 [256, 8, 16, 640], P(('rep', 'fsdp'))
- shortcut: bfloat16 [256, 8, 16, 640], P(('rep', 'fsdp'))
- grad_down: float32 [2880, 320], P('fsdp')
- grad_conv: float32 [2880, 640], P('fsdp')
- grad_skip: float32 [320, 640], P('fsdp')
The draws below stay inside these ranges and needn't reach their ends.
All inputs are finite; a program needn't handle non-finite values.
Results may differ from the reference program's by a relative error of at most 0.029.
Values may be sent and summed in bfloat16 or wider, within the bound.
A program may use at most 128 MiB of HBM per device.

```python
import jax
import jax.numpy as jnp
from jax import lax

C0 = 320
C1 = 640
GROUPS = 32
RH = 8
RW = 16
IMAGES = 256


def steps_of(stream_key, shape, split, least, largest):
    loudness, own = 1.0, jax.random.fold_in(stream_key, 6)
    for position, blocks in split:
        draws = jnp.exp(jax.random.uniform(jax.random.fold_in(own, position), (blocks,), jnp.float32, least / len(split), largest / len(split)))
        loudness = loudness * jnp.repeat(draws, shape[position] // blocks).reshape([-1 if axis == position else 1 for axis in range(len(shape))])
    return loudness


def noise(own_key, shape, scale, bound, split=(), held_as=jnp.bfloat16):
    values = jax.random.normal(own_key, shape, jnp.float32) * scale
    if len(split) > 0:
        values = steps_of(own_key, shape, split, -0.22, 0.18) * values
    return jnp.clip(values, min=-bound, max=bound).astype(held_as)


def setup_inputs(seed: int = 0) -> dict:
    splits = jax.random.split(jax.random.key(seed), 7)
    images = noise(splits[0], (IMAGES, 2 * RH, 2 * RW, C0), 1.0, 6.0, ((0, 256),))
    w_down = noise(splits[1], (9 * C0, C0), (9 * C0) ** -0.5, 0.109375, ((0, 32),))
    w_conv = noise(splits[2], (9 * C0, C1), (9 * C0) ** -0.5, 0.109375, ((0, 32),))
    w_skip = noise(splits[3], (C0, C1), C0 ** -0.5, 0.3125, ((0, 32),))
    act_grad = noise(splits[4], (IMAGES, RH, RW, C1), 1.0, 6.0, ((0, 256),))
    short_grad = noise(splits[5], (IMAGES, RH, RW, C1), 1.0, 6.0, ((0, 256),))
    return {"images": images, "w_down": w_down, "w_conv": w_conv, "w_skip": w_skip, "act_grad": act_grad, "short_grad": short_grad}


def norm_silu(values):
    grouped = values.reshape(values.shape[0], values.shape[1] * values.shape[2], GROUPS, values.shape[3] // GROUPS)
    average = lax.optimization_barrier(jnp.mean(grouped, axis=(1, 3), keepdims=True))
    centred = grouped - average
    spread = lax.optimization_barrier(jnp.mean(centred * centred, axis=(1, 3), keepdims=True))
    normed = centred * lax.rsqrt(spread + 1e-05)
    return jax.nn.silu(normed).reshape(values.shape)

def convolve(inputs, weight, stride):
    kernel = weight.reshape(3, 3, inputs.shape[3], weight.shape[1])
    return lax.conv_general_dilated(inputs, kernel, (stride, stride), ((1, 1), (1, 1)), dimension_numbers=('NHWC', 'HWIO', 'NHWC'), preferred_element_type=jnp.float32)

def forward(pictures, w_down, w_conv, w_skip):
    reduced = convolve(pictures, w_down, 2).astype(jnp.bfloat16)
    first = norm_silu(reduced.astype(jnp.float32)).astype(jnp.bfloat16)
    hidden = convolve(first, w_conv, 1).astype(jnp.bfloat16)
    activated = norm_silu(hidden.astype(jnp.float32)).astype(jnp.bfloat16)
    shortcut = jnp.dot(reduced, w_skip, preferred_element_type=jnp.float32).astype(jnp.bfloat16)
    return (activated, shortcut)

def reference(images, w_down, w_conv, w_skip, act_grad, short_grad):

    def per_image(totals, element):
        picture, act_cot, short_cot = element

        def local_forward(kernel_down, kernel_conv, kernel_skip):
            return forward(picture[None], kernel_down, kernel_conv, kernel_skip)
        outputs, pullback = jax.vjp(local_forward, w_down, w_conv, w_skip)
        gradients = pullback((act_cot[None], short_cot[None]))
        totals = tuple((total + grad.astype(jnp.float32) for total, grad in zip(totals, gradients)))
        return (totals, (outputs[0][0], outputs[1][0]))
    initial = tuple((jnp.zeros(weight.shape, jnp.float32) for weight in (w_down, w_conv, w_skip)))
    summed, stacked = lax.scan(per_image, initial, (images, act_grad, short_grad))
    inverse = 1.0 / images.shape[0]
    return (stacked[0], stacked[1], summed[0] * inverse, summed[1] * inverse, summed[2] * inverse)
```

```python
import jax
import jax.numpy as jnp
from jax import lax
from jax.experimental import pallas as pl
from jax.experimental.pallas import tpu as pltpu
from jax.sharding import PartitionSpec as P

MESH = pl.DeviceIdType.MESH
BF = jnp.bfloat16
F32 = jnp.float32

C0, C1 = 320, 640
LANES0 = 384
SHARD = 90
PAD = 96
SKIP, SKIP_PAD = 10, 16
ROWS_A, ROWS_B = PAD, PAD + SKIP_PAD
HALF_A, HALF_B = 48, 64
PART = 32
CELLS = 128
TILE = 256
COLS = 32 * PAD
CHUNK = 8 * PAD
SEMS = 160
EPS = 1e-5


def source_of(col):
    shard, place = divmod(col, PAD)
    return SHARD * shard + place if place < SHARD else -1


def tile_taps():
    pairs = []
    for tile in range(COLS // TILE):
        cols = [source_of(c) for c in range(tile * TILE, (tile + 1) * TILE)]
        for tap in sorted({s // C0 for s in cols if s >= 0}):
            pairs.append((tile, tap))
    return pairs


PAIRS = tile_taps()


def iota(shape, axis):
    return lax.broadcasted_iota(jnp.int32, shape, axis)


def ones_where(mask):
    return jnp.where(mask, 1.0, 0.0).astype(BF)


def spread_matrix(tile, tap):
    lane = iota((1, TILE), 1) + tile * TILE
    shard = jnp.full((1, TILE), tile * TILE // PAD, jnp.int32)
    for edge in range(PAD, COLS, PAD):
        if tile * TILE < edge < (tile + 1) * TILE:
            shard = shard + jnp.where(lane >= edge, 1, 0)
    place = lane - PAD * shard
    channel = lane - (PAD - SHARD) * shard - C0 * tap
    good = (place < SHARD) & (channel >= 0) & (channel < C0)
    channel = jnp.where(good, channel, -1)
    return ones_where(iota((LANES0, TILE), 0) == channel)


def skip_matrix():
    lane = iota((1, 32 * SKIP_PAD), 1)
    shard = lane >> 4
    place = lane - SKIP_PAD * shard
    channel = jnp.where(place < SKIP, SKIP * shard + place, -1)
    return ones_where(iota((LANES0, 32 * SKIP_PAD), 0) == channel)


def shift_down(tap):
    kh, kw = divmod(tap, 3)
    cell = iota((CELLS, 1), 0)
    row, col = 2 * (cell >> 4) + kh - 1, 2 * (cell & 15) + kw - 1
    index = jnp.where((row >= 0) & (col >= 0), row * 32 + col, -1)
    return ones_where(iota((CELLS, 512), 1) == index)


def shift_conv(tap):
    kh, kw = divmod(tap, 3)
    cell = iota((CELLS, 1), 0)
    row, col = (cell >> 4) + kh - 1, (cell & 15) + kw - 1
    good = (row >= 0) & (row < 8) & (col >= 0) & (col < 16)
    index = jnp.where(good, row * 16 + col, -1)
    return ones_where(iota((CELLS, CELLS), 1) == index)


def dot(a, b):
    return lax.dot_general(a, b, (((1,), (0,)), ((), ())), preferred_element_type=F32)


def dot_nt(a, b):
    return lax.dot_general(a, b, (((1,), (1,)), ((), ())), preferred_element_type=F32)


def dot_tn(a, b):
    return lax.dot_general(a, b, (((0,), (0,)), ((), ())), preferred_element_type=F32)


def group_matrix(width, group_of):
    return ones_where(group_of(iota((width, width), 0)) == group_of(iota((width, width), 1)))


def group10(c):
    return (c * 6554) >> 16


def group20(c):
    return (c * 3277) >> 16


def group_sums(vectors, same):
    width = same.shape[0]
    row = iota((8, width), 0)
    stacked = jnp.zeros((8, width), F32)
    for number, vector in enumerate(vectors):
        rest = vector
        for term in range(3):
            part = rest.astype(BF).astype(F32)
            rest = rest - part
            stacked = jnp.where(row == 4 * number + term, part, stacked)
    sums = dot(stacked.astype(BF), same)
    return [jnp.sum(sums[4 * n : 4 * n + 4], axis=0, keepdims=True) for n in range(len(vectors))]


def normalise(values, same, count):
    (total,) = group_sums([jnp.sum(values, axis=0, keepdims=True)], same)
    centred = values - total * (1.0 / count)
    (square,) = group_sums([jnp.sum(centred * centred, axis=0, keepdims=True)], same)
    scale = lax.rsqrt(square * (1.0 / count) + EPS)
    return centred * scale, scale


def normalise_back(cotangent, normed, scale, same, count):
    sig = 1.0 / (1.0 + jnp.exp(-normed))
    slope = cotangent * (sig * (1.0 + normed * (1.0 - sig)))
    first, second = group_sums(
        [jnp.sum(slope, axis=0, keepdims=True), jnp.sum(slope * normed, axis=0, keepdims=True)], same
    )
    return scale * (slope - first * (1.0 / count) - normed * (second * (1.0 / count)))


def silu(normed):
    return normed / (1.0 + jnp.exp(-normed))


class Copies:
    def __init__(self, send, recv):
        self.send, self.recv, self.started = send, recv, []

    def start(self, src, dst, device):
        number = len(self.started)
        copy = pltpu.make_async_remote_copy(
            src_ref=src,
            dst_ref=dst,
            send_sem=self.send.at[number],
            recv_sem=self.recv.at[number],
            device_id=device,
            device_id_type=MESH,
        )
        copy.start()
        self.started.append(copy)
        return copy


class Gather:
    def __init__(self, copies, piece, place, after, before):
        self.copies, self.piece, self.place = copies, piece, place
        self.after, self.before = after, before

    def send(self, chunk, half, device):
        ref = self.piece(chunk, half)
        return self.copies.start(ref, ref, device)

    def start(self):
        self.first = self.send(self.place, None, self.after)
        self.second = self.send(self.place, None, self.before)

    def forward(self):
        self.first.wait_recv()
        self.third = self.send((self.place + 3) % 4, 0, self.after)
        self.second.wait_recv()
        self.fourth = self.send((self.place + 1) % 4, 1, self.before)

    def finish(self):
        self.third.wait_recv()
        self.fourth.wait_recv()


def add_into(ref, *others):
    total = ref[...].astype(F32)
    for other in others:
        total = total + other[...].astype(F32)
    ref[...] = total.astype(BF)


class Scatter:
    def __init__(self, copies, piece, place, after, before, lands):
        self.copies, self.piece, self.place = copies, piece, place
        self.after, self.before, self.lands = after, before, lands

    def send(self, chunk, half, slot, device):
        return self.copies.start(self.piece(chunk % 4, half), self.lands[half].at[slot], device)

    def start(self):
        p = self.place
        self.c0 = self.send(p + 2, 0, 0, self.after)
        self.c1 = self.send(p + 2, 1, 0, self.before)
        self.c2 = self.send(p + 1, 1, 1, self.after)
        self.c3 = self.send(p + 3, 0, 1, self.before)

    def middle(self):
        p = self.place
        self.c0.wait_recv()
        add_into(self.piece((p + 1) % 4, 0), self.lands[0].at[0])
        self.c4 = self.send(p + 1, 0, 2, self.after)
        self.c1.wait_recv()
        add_into(self.piece((p + 3) % 4, 1), self.lands[1].at[0])
        self.c5 = self.send(p + 3, 1, 2, self.before)

    def finish(self):
        self.c2.wait_recv()
        self.c3.wait_recv()
        self.c4.wait_recv()
        add_into(self.piece(self.place, 0), self.lands[0].at[1], self.lands[0].at[2])
        self.c5.wait_recv()
        add_into(self.piece(self.place, 1), self.lands[1].at[1], self.lands[1].at[2])


def kernel(
    img, wd, wc, ws, ag, sg,
    act_out, short_out, down_out, conv_out, skip_out,
    ga, gb, grad_a, grad_b, sib_a, sib_b, sum_a, sum_b,
    a0y, a1z, a0z0, a0z1, a1y0, a1y1,
    b0y, b1z, b0z0, b0z1, b1y0, b1y1,
    share, share_in, share_z, full,
    spread, padded_img, taps, cols_img, cols_first,
    send, recv,
):
    rep, shard = lax.axis_index("rep"), lax.axis_index("fsdp")
    x, y, zl, core = rep % 4, shard // 8, (shard // 2) % 4, shard % 2
    z = (rep // 4) * 4 + zl

    def device(x, y, z, core):
        return ((z // 4) * 4 + x, (y * 4 + z % 4) * 2 + core)

    sibling = device(x, y, z, 1 - core)
    y_next, y_prev = device(x, (y + 1) % 4, z, core), device(x, (y + 3) % 4, z, core)
    z_next, z_prev = device(x, y, (z + 1) % 8, core), device(x, y, (z + 7) % 8, core)
    z_far = device(x, y, (z + 4) % 8, core)
    x_others = [device((x + d) % 4, y, z, core) for d in (1, 2, 3)]

    ga[y, zl, core] = jnp.zeros((ROWS_A, LANES0), BF)
    ga[y, zl, core, 0:SHARD, 0:C0] = wd[...]
    gb[y, zl, core] = jnp.zeros((ROWS_B, C1), BF)
    gb[y, zl, core, 0:SHARD] = wc[...]
    gb[y, zl, core, PAD : PAD + SKIP] = ws[...]

    barrier = pltpu.get_barrier_semaphore()
    greeted = [sibling, y_next, y_prev, z_next, z_prev, z_far] + x_others
    for other in greeted:
        pl.semaphore_signal(barrier, inc=1, device_id=other, device_id_type=MESH)
    pl.semaphore_wait(barrier, len(greeted))

    copies = Copies(send, recv)

    some = {None: pl.ds(0, 4), 0: pl.ds(0, 2), 1: pl.ds(2, 2)}

    def rows_of(half, low, high):
        return {None: pl.ds(low, high - low), 0: pl.ds(low, PART), 1: pl.ds(low + PART, high - low - PART)}[half]

    def gather_of(buf, rows, half_rows):
        low, high = (0, half_rows), (half_rows, rows)
        one0 = Gather(copies, lambda c, h: buf.at[y, c, core, rows_of(h, *low)], zl, z_next, z_prev)
        one1 = Gather(copies, lambda c, h: buf.at[c, zl, core, rows_of(h, *high)], y, y_next, y_prev)
        two0 = Gather(copies, lambda c, h: buf.at[c, some[h], core, rows_of(None, *low)], y, y_next, y_prev)
        two1 = Gather(copies, lambda c, h: buf.at[some[h], c, core, rows_of(None, *high)], zl, z_next, z_prev)
        return (one0, one1), (two0, two1)

    one_a, two_a = gather_of(ga, ROWS_A, HALF_A)
    one_b, two_b = gather_of(gb, ROWS_B, HALF_B)
    to_sibling = {"a": [], "b": []}

    def share_with_sibling(name, ring, offset):
        ref = ring.piece((ring.place + offset) % 4, None)
        to_sibling[name].append(copies.start(ref, ref, sibling))

    for ring in one_a + one_b:
        ring.start()

    for number, (tile, tap) in enumerate(PAIRS):
        spread[number] = spread_matrix(tile, tap)
    padded_img[...] = jnp.zeros((512, LANES0), BF)
    padded_img[:, 0:C0] = img[...]

    for ring in one_a + one_b:
        ring.forward()

    def columns(out):
        for tile in range(COLS // TILE):
            total = None
            for number, (tile_of, tap) in enumerate(PAIRS):
                if tile_of == tile:
                    term = dot(taps[tap], spread[number])
                    total = term if total is None else total + term
            out[:, tile * TILE : (tile + 1) * TILE] = total.astype(BF)

    for ring in one_a:
        ring.finish()
    for ring in two_a:
        ring.start()
    for ring in two_a:
        share_with_sibling("a", ring, 0)
    for ring in one_b:
        ring.finish()
    for ring in two_b:
        ring.start()
    for ring in two_b:
        share_with_sibling("b", ring, 0)

    for tap in range(9):
        taps[tap] = dot(shift_down(tap), padded_img[...]).astype(BF)

    for ring in two_a:
        ring.forward()
    for ring in two_a:
        share_with_sibling("a", ring, 1)
        share_with_sibling("a", ring, 3)

    columns(cols_img)

    for ring in two_a:
        ring.finish()
        share_with_sibling("a", ring, 2)
    for ring in two_b:
        ring.forward()
    for ring in two_b:
        share_with_sibling("b", ring, 1)
        share_with_sibling("b", ring, 3)
    for copy in to_sibling["a"]:
        copy.wait_recv()

    def chunk_of(q):
        return slice(q * CHUNK, (q + 1) * CHUNK)

    def down_rows(q):
        return ga[q].reshape(CHUNK, LANES0)

    def conv_rows(q):
        return gb[q, :, :, 0:PAD, :].reshape(CHUNK, C1)

    reduced = sum(dot(cols_img[:, chunk_of(q)], down_rows(q)) for q in range(4)).astype(BF)
    same0 = group_matrix(LANES0, group10)
    normed0, scale0 = normalise(reduced.astype(F32), same0, CELLS * (C0 // 32))
    first = silu(normed0).astype(BF)
    for tap in range(9):
        taps[tap] = dot(shift_conv(tap), first).astype(BF)
    columns(cols_first)
    skip_spread = skip_matrix()
    reduced_cols = dot(reduced, skip_spread).astype(BF)
    grad_b[:, :, :, PAD:ROWS_B, :] = dot_tn(reduced_cols, sg[...]).astype(BF).reshape(4, 4, 2, SKIP_PAD, C1)

    for ring in two_b:
        ring.finish()
        share_with_sibling("b", ring, 2)
    for copy in to_sibling["b"]:
        copy.wait_recv()

    hidden = sum(dot(cols_first[:, chunk_of(q)], conv_rows(q)) for q in range(4)).astype(BF)
    same1 = group_matrix(C1, group20)
    normed1, scale1 = normalise(hidden.astype(F32), same1, CELLS * (C1 // 32))
    act_out[...] = silu(normed1).astype(BF)
    d_hidden = normalise_back(ag[...].astype(F32), normed1, scale1, same1, CELLS * (C1 // 32)).astype(BF)

    from_sibling = {"a": [], "b": []}

    def to_other_core(name, grads, lands, q):
        from_sibling[name].append(copies.start(grads.at[q, :, 1 - core], lands.at[q], sibling))

    def add_cores(name, grads, lands, sums):
        for q in range(4):
            from_sibling[name][q].wait_recv()
            sums[q] = (grads[q, :, core].astype(F32) + lands[q].astype(F32)).astype(BF)

    for q in range(4):
        part = dot_tn(cols_first[:, chunk_of(q)], d_hidden).astype(BF)
        grad_b[q, :, :, 0:PAD, :] = part.reshape(4, 2, PAD, C1)
        to_other_core("b", grad_b, sib_b, q)

    def scatter_of(buf, rows, half_rows, lands0y, lands1z, lands0z, lands1y):
        low, high = (0, half_rows), (half_rows, rows)
        one0 = Scatter(copies, lambda c, h: buf.at[c, some[h], rows_of(None, *low)], y, y_next, y_prev,
                       (lands0y.at[0], lands0y.at[1]))
        one1 = Scatter(copies, lambda c, h: buf.at[some[h], c, rows_of(None, *high)], zl, z_next, z_prev,
                       (lands1z.at[0], lands1z.at[1]))
        two0 = Scatter(copies, lambda c, h: buf.at[y, c, rows_of(h, *low)], zl, z_next, z_prev, lands0z)
        two1 = Scatter(copies, lambda c, h: buf.at[c, zl, rows_of(h, *high)], y, y_next, y_prev, lands1y)
        return (one0, one1), (two0, two1)

    down_a, down2_a = scatter_of(sum_a, ROWS_A, HALF_A, a0y, a1z, (a0z0, a0z1), (a1y0, a1y1))
    down_b, down2_b = scatter_of(sum_b, ROWS_B, HALF_B, b0y, b1z, (b0z0, b0z1), (b1y0, b1y1))

    for q in range(4):
        cols_first[:, chunk_of(q)] = dot_nt(d_hidden, conv_rows(q)).astype(BF)

    add_cores("b", grad_b, sib_b, sum_b)
    for ring in down_b:
        ring.start()

    d_first = jnp.zeros((CELLS, LANES0), F32)
    for tap in range(9):
        part = None
        for number, (tile, tap_of) in enumerate(PAIRS):
            if tap_of == tap:
                term = dot_nt(cols_first[:, tile * TILE : (tile + 1) * TILE], spread[number])
                part = term if part is None else part + term
        d_first = d_first + dot(shift_conv(8 - tap), part.astype(BF))

    skip_rows = gb[:, :, :, PAD:ROWS_B, :].reshape(32 * SKIP_PAD, C1)
    short_out[...] = dot(reduced_cols, skip_rows).astype(BF)
    d_skip = dot_nt(dot_nt(sg[...], skip_rows).astype(BF), skip_spread)
    d_norm = normalise_back(
        d_first.astype(BF).astype(F32), normed0, scale0, same0, CELLS * (C0 // 32)
    )
    d_reduced = (d_norm + d_skip).astype(BF)

    for q in range(4):
        part = dot_tn(cols_img[:, chunk_of(q)], d_reduced).astype(BF)
        grad_a[q] = part.reshape(4, 2, PAD, LANES0)
        to_other_core("a", grad_a, sib_a, q)

    for ring in down_b:
        ring.middle()
    add_cores("a", grad_a, sib_a, sum_a)
    for ring in down_a:
        ring.start()
    for ring in down_b:
        ring.finish()
    for ring in down2_b:
        ring.start()
    for ring in down_a:
        ring.middle()
    for ring in down2_b:
        ring.middle()
    for ring in down_a:
        ring.finish()
    for ring in down2_a:
        ring.start()
    for ring in down2_b:
        ring.finish()
    for ring in down2_a:
        ring.middle()
    for ring in down2_a:
        ring.finish()

    for tile in range(5):
        share[tile] = sum_b[y, zl, :, tile * 128 : (tile + 1) * 128]
    for tile in range(3):
        share[5 + tile] = jnp.zeros((ROWS_B, 128), BF)
        share[5 + tile, 0:PAD] = sum_a[y, zl, :, tile * 128 : (tile + 1) * 128]
    spread_out = [
        copies.start(share.at[pl.ds(2 * ((x + d) % 4), 2)], share_in.at[d - 1], x_others[d - 1])
        for d in (1, 2, 3)
    ]
    for copy in spread_out:
        copy.wait_recv()
    total = share[pl.ds(2 * x, 2)].astype(F32)
    for slot in range(3):
        total = total + share_in[slot].astype(F32)
    share_z[0] = total.astype(BF)
    copy = copies.start(share_z.at[0], share_z.at[1], z_far)
    copy.wait_recv()
    full[pl.ds(2 * x, 2)] = (share_z[0].astype(F32) + share_z[1].astype(F32)).astype(BF)
    mine = full.at[pl.ds(2 * x, 2)]
    gathered = [copies.start(mine, mine, other) for other in x_others]
    for copy in gathered:
        copy.wait_recv()

    inverse = 1.0 / 256
    for tile in range(5):
        lanes = slice(tile * 128, (tile + 1) * 128)
        values = full[tile].astype(F32) * inverse
        conv_out[:, lanes] = values[0:SHARD]
        skip_out[:, lanes] = values[PAD : PAD + SKIP]
    for tile in range(3):
        high = min(C0, (tile + 1) * 128)
        values = full[5 + tile].astype(F32) * inverse
        down_out[:, tile * 128 : high] = values[0:SHARD, 0 : high - tile * 128]

    for copy in copies.started:
        copy.wait_send()


def vmem(*shape):
    return pltpu.VMEM(shape, BF)


def body(images, w_down, w_conv, w_skip, act_grad, short_grad):
    picture = images.reshape(512, C0)
    act_cot = act_grad.reshape(CELLS, C1)
    short_cot = short_grad.reshape(CELLS, C1)

    def lands(lanes, low, high):
        return [
            vmem(2, 3, 2, low, lanes),
            vmem(2, 3, 2, high, lanes),
            vmem(3, PART, lanes),
            vmem(3, low - PART, lanes),
            vmem(3, PART, lanes),
            vmem(3, high - PART, lanes),
        ]

    outs = pl.pallas_call(
        kernel,
        out_shape=(
            jax.ShapeDtypeStruct((CELLS, C1), BF),
            jax.ShapeDtypeStruct((CELLS, C1), BF),
            jax.ShapeDtypeStruct((SHARD, C0), F32),
            jax.ShapeDtypeStruct((SHARD, C1), F32),
            jax.ShapeDtypeStruct((SKIP, C1), F32),
        ),
        in_specs=[pl.BlockSpec(memory_space=pltpu.VMEM)] * 6,
        out_specs=tuple([pl.BlockSpec(memory_space=pltpu.VMEM)] * 5),
        scratch_shapes=[
            vmem(4, 4, 2, ROWS_A, LANES0),
            vmem(4, 4, 2, ROWS_B, C1),
            vmem(4, 4, 2, ROWS_A, LANES0),
            vmem(4, 4, 2, ROWS_B, C1),
            vmem(4, 4, ROWS_A, LANES0),
            vmem(4, 4, ROWS_B, C1),
            vmem(4, 4, ROWS_A, LANES0),
            vmem(4, 4, ROWS_B, C1),
            *lands(LANES0, HALF_A, ROWS_A - HALF_A),
            *lands(C1, HALF_B, ROWS_B - HALF_B),
            vmem(8, ROWS_B, 128),
            vmem(3, 2, ROWS_B, 128),
            vmem(2, 2, ROWS_B, 128),
            vmem(8, ROWS_B, 128),
            vmem(len(PAIRS), LANES0, TILE),
            vmem(512, LANES0),
            vmem(9, CELLS, LANES0),
            vmem(CELLS, COLS),
            vmem(CELLS, COLS),
            pltpu.SemaphoreType.DMA((SEMS,)),
            pltpu.SemaphoreType.DMA((SEMS,)),
        ],
        compiler_params=pltpu.CompilerParams(
            collective_id=0, has_side_effects=True, vmem_limit_bytes=56 * 1024 * 1024
        ),
    )(picture, w_down, w_conv, w_skip, act_cot, short_cot)
    activated, shortcut, down, conv, skip = outs
    return (
        activated.reshape(act_grad.shape),
        shortcut.reshape(short_grad.shape),
        down,
        conv,
        skip,
    )


def solution(mesh):
    cells = P(("rep", "fsdp"), None, None, None)
    rows = P("fsdp", None)
    return jax.shard_map(
        body,
        mesh=mesh,
        in_specs=(cells, rows, rows, rows, cells, cells),
        out_specs=(cells, cells, rows, rows, rows),
        check_vma=False,
    )
```

```python
import jax
import jax.numpy as jnp
from jax import lax
from jax.experimental import pallas as pl
from jax.experimental.pallas import tpu as pltpu
from jax.sharding import PartitionSpec as P

MESH = pl.DeviceIdType.MESH
BF = jnp.bfloat16
F32 = jnp.float32

C0, C1 = 320, 640
LANES0 = 384
SHARD = 90
PAD = 96
SKIP, SKIP_PAD = 10, 16
ROW_TILES = PAD // 16
CELLS = 128
TILE = 256
COLS = 32 * PAD
CHUNK = 8 * PAD
SEMS = 240
EPS = 1e-5


def source_of(col):
    shard, place = divmod(col, PAD)
    return SHARD * shard + place if place < SHARD else -1


def tile_taps():
    pairs = []
    for tile in range(COLS // TILE):
        cols = [source_of(c) for c in range(tile * TILE, (tile + 1) * TILE)]
        for tap in sorted({s // C0 for s in cols if s >= 0}):
            pairs.append((tile, tap))
    return pairs


PAIRS = tile_taps()


def iota(shape, axis):
    return lax.broadcasted_iota(jnp.int32, shape, axis)


def ones_where(mask):
    return jnp.where(mask, 1.0, 0.0).astype(BF)


def spread_matrix(tile, tap):
    lane = iota((1, TILE), 1) + tile * TILE
    shard = jnp.full((1, TILE), tile * TILE // PAD, jnp.int32)
    for edge in range(PAD, COLS, PAD):
        if tile * TILE < edge < (tile + 1) * TILE:
            shard = shard + jnp.where(lane >= edge, 1, 0)
    place = lane - PAD * shard
    channel = lane - (PAD - SHARD) * shard - C0 * tap
    good = (place < SHARD) & (channel >= 0) & (channel < C0)
    channel = jnp.where(good, channel, -1)
    return ones_where(iota((LANES0, TILE), 0) == channel)


def skip_matrix():
    lane = iota((1, 32 * SKIP_PAD), 1)
    shard = lane >> 4
    place = lane - SKIP_PAD * shard
    channel = jnp.where(place < SKIP, SKIP * shard + place, -1)
    return ones_where(iota((LANES0, 32 * SKIP_PAD), 0) == channel)


def shift_down(tap):
    kh, kw = divmod(tap, 3)
    cell = iota((CELLS, 1), 0)
    row, col = 2 * (cell >> 4) + kh - 1, 2 * (cell & 15) + kw - 1
    index = jnp.where((row >= 0) & (col >= 0), row * 32 + col, -1)
    return ones_where(iota((CELLS, 512), 1) == index)


def shift_conv(tap):
    kh, kw = divmod(tap, 3)
    cell = iota((CELLS, 1), 0)
    row, col = (cell >> 4) + kh - 1, (cell & 15) + kw - 1
    good = (row >= 0) & (row < 8) & (col >= 0) & (col < 16)
    index = jnp.where(good, row * 16 + col, -1)
    return ones_where(iota((CELLS, CELLS), 1) == index)


def dot(a, b):
    return lax.dot_general(a, b, (((1,), (0,)), ((), ())), preferred_element_type=F32)


def dot_nt(a, b):
    return lax.dot_general(a, b, (((1,), (1,)), ((), ())), preferred_element_type=F32)


def dot_tn(a, b):
    return lax.dot_general(a, b, (((0,), (0,)), ((), ())), preferred_element_type=F32)


def group_matrix(width, group_of):
    return ones_where(group_of(iota((width, width), 0)) == group_of(iota((width, width), 1)))


def group10(c):
    return (c * 6554) >> 16


def group20(c):
    return (c * 3277) >> 16


def group_sums(vectors, same):
    width = same.shape[0]
    row = iota((8, width), 0)
    stacked = jnp.zeros((8, width), F32)
    for number, vector in enumerate(vectors):
        rest = vector
        for term in range(3):
            part = rest.astype(BF).astype(F32)
            rest = rest - part
            stacked = jnp.where(row == 4 * number + term, part, stacked)
    sums = dot(stacked.astype(BF), same)
    return [jnp.sum(sums[4 * n : 4 * n + 4], axis=0, keepdims=True) for n in range(len(vectors))]


def normalise(values, same, count):
    (total,) = group_sums([jnp.sum(values, axis=0, keepdims=True)], same)
    centred = values - total * (1.0 / count)
    (square,) = group_sums([jnp.sum(centred * centred, axis=0, keepdims=True)], same)
    scale = lax.rsqrt(square * (1.0 / count) + EPS)
    return centred * scale, scale


def normalise_back(cotangent, normed, scale, same, count):
    sig = 1.0 / (1.0 + jnp.exp(-normed))
    slope = cotangent * (sig * (1.0 + normed * (1.0 - sig)))
    first, second = group_sums(
        [jnp.sum(slope, axis=0, keepdims=True), jnp.sum(slope * normed, axis=0, keepdims=True)], same
    )
    return scale * (slope - first * (1.0 / count) - normed * (second * (1.0 / count)))


def silu(normed):
    return normed / (1.0 + jnp.exp(-normed))


class Tiles:
    def __init__(self, quarter, middle, end, slots):
        self.quarter, self.middle, self.end, self.slots = quarter, middle, end, slots
        self.from1 = 4 * quarter
        self.from2 = self.from1 + middle
        self.count1, self.count2 = middle, end
        self.rest = (slots - self.from1) // 4
        self.own = quarter + self.rest

    def place(self, tile):
        if tile < self.from1:
            return tile // self.quarter, tile % self.quarter
        tile -= self.from1
        return tile // self.rest, self.quarter + tile % self.rest


TILES_A = Tiles(2, 4, 6, 20)
TILES_B = Tiles(4, 12, 7, 36)

ALL, LOW, HIGH = pl.ds(0, 4), pl.ds(0, 2), pl.ds(2, 2)
SOME = {None: ALL, 0: LOW, 1: HIGH}


def part_of(start, count, half):
    first = (count + 1) // 2
    if half is None:
        return pl.ds(start, count)
    return pl.ds(start, first) if half == 0 else pl.ds(start + first, count - first)


def part_size(count, half):
    return (count + 1) // 2 if half == 0 else count // 2


class Copies:
    def __init__(self, send, recv):
        self.send, self.recv, self.started = send, recv, []

    def start(self, src, dst, device):
        number = len(self.started)
        copy = pltpu.make_async_remote_copy(
            src_ref=src,
            dst_ref=dst,
            send_sem=self.send.at[number],
            recv_sem=self.recv.at[number],
            device_id=device,
            device_id_type=MESH,
        )
        copy.start()
        self.started.append(copy)
        return copy


class Gather:
    def __init__(self, copies, piece, ring):
        self.copies, self.piece = copies, piece
        self.place, self.after, self.before = ring

    def send(self, chunk, half, device):
        ref = self.piece(chunk, half)
        return self.copies.start(ref, ref, device)

    def start(self):
        self.first = self.send(self.place, None, self.after)
        self.second = self.send(self.place, None, self.before)

    def forward(self):
        self.first.wait_recv()
        self.third = self.send((self.place + 3) % 4, 0, self.after)
        self.second.wait_recv()
        self.fourth = self.send((self.place + 1) % 4, 1, self.before)

    def finish(self):
        self.third.wait_recv()
        self.fourth.wait_recv()


def add_into(ref, *others):
    total = ref[...].astype(F32)
    for other in others:
        total = total + other[...].astype(F32)
    ref[...] = total.astype(BF)


class Scatter:
    def __init__(self, copies, piece, ring, lands):
        self.copies, self.piece = copies, piece
        self.place, self.after, self.before = ring
        self.lands = lands

    def send(self, chunk, half, slot, device):
        return self.copies.start(self.piece(chunk % 4, half), self.lands[half].at[slot], device)

    def start(self):
        p = self.place
        self.c0 = self.send(p + 2, 0, 0, self.after)
        self.c1 = self.send(p + 2, 1, 0, self.before)
        self.c2 = self.send(p + 1, 1, 1, self.after)
        self.c3 = self.send(p + 3, 0, 1, self.before)

    def middle(self):
        p = self.place
        self.c0.wait_recv()
        add_into(self.piece((p + 1) % 4, 0), self.lands[0].at[0])
        self.c4 = self.send(p + 1, 0, 2, self.after)
        self.c1.wait_recv()
        add_into(self.piece((p + 3) % 4, 1), self.lands[1].at[0])
        self.c5 = self.send(p + 3, 1, 2, self.before)

    def finish(self):
        self.c2.wait_recv()
        self.c3.wait_recv()
        self.c4.wait_recv()
        add_into(self.piece(self.place, 0), self.lands[0].at[1], self.lands[0].at[2])
        self.c5.wait_recv()
        add_into(self.piece(self.place, 1), self.lands[1].at[1], self.lands[1].at[2])


def scatter_slots(cut):
    shapes = []
    for shape in ((2, 4, cut.quarter), (2, cut.count1), (2, cut.count2), (2, cut.quarter)):
        shapes.append([shape] * 2)
    for size in (cut.count1, cut.count2, cut.quarter, cut.rest):
        shapes.append([(part_size(size, 0),), (part_size(size, 1),)])
    return shapes


def each(method, *rings):
    for ring in rings:
        getattr(ring, method)()


class Weights:
    def __init__(self, copies, buf, cut, at, rings, sibling):
        x, y, zl, core = at
        on_x, on_y, on_z = rings
        mine = cut.quarter * x
        quarter, one, two = cut.quarter, cut.from1, cut.from2
        n1, n2 = cut.count1, cut.count2
        self.copies, self.sibling, self.shared = copies, sibling, []
        self.first = (
            Gather(copies, lambda c, h: buf.at[y, c, core, part_of(mine, quarter, h)], on_z),
            Gather(copies, lambda c, h: buf.at[y, c, core, part_of(one, n1, h)], on_z),
            Gather(copies, lambda c, h: buf.at[c, zl, core, part_of(two, n2, h)], on_y),
        )
        self.second = (
            Gather(copies, lambda c, h: buf.at[c, SOME[h], core, part_of(mine, quarter, None)], on_y),
            Gather(copies, lambda c, h: buf.at[c, SOME[h], core, part_of(one, n1, None)], on_y),
            Gather(copies, lambda c, h: buf.at[SOME[h], c, core, part_of(two, n2, None)], on_z),
        )
        self.third = Gather(copies, lambda c, h: buf.at[SOME[h], ALL, core, part_of(quarter * c, quarter, None)], on_x)

    def share(self, rings, *offsets):
        for ring in rings:
            for offset in offsets:
                ref = ring.piece((ring.place + offset) % 4, None)
                self.shared.append(self.copies.start(ref, ref, self.sibling))

    def wait_shared(self):
        for copy in self.shared:
            copy.wait_recv()


class Gradients:
    def __init__(self, copies, grads, lands, sums, slots, ends, cut, at, rings, devices):
        x, y, zl, core = at
        on_x, on_y, on_z = rings
        self.copies, self.grads, self.lands, self.sums, self.cut, self.at = copies, grads, lands, sums, cut, at
        self.own, self.far, self.full = ends
        self.sibling, self.z_far, self.x_others = devices
        self.crossed = []
        mine = cut.quarter * x
        quarter, one, two, rest = cut.quarter, cut.from1, cut.from2, cut.rest
        n1, n2 = cut.count1, cut.count2
        pairs = [slots[2 * i : 2 * i + 2] for i in range(8)]
        self.first = (
            Scatter(copies, lambda c, h: sums.at[SOME[h], ALL, part_of(quarter * c, quarter, None)], on_x, pairs[0]),
            Scatter(copies, lambda c, h: sums.at[c, SOME[h], part_of(one, n1, None)], on_y, pairs[1]),
            Scatter(copies, lambda c, h: sums.at[SOME[h], c, part_of(two, n2, None)], on_z, pairs[2]),
        )
        self.second = (
            Scatter(copies, lambda c, h: sums.at[c, SOME[h], part_of(mine, quarter, None)], on_y, pairs[3]),
            Scatter(copies, lambda c, h: sums.at[y, c, part_of(one, n1, h)], on_z, pairs[4]),
            Scatter(copies, lambda c, h: sums.at[c, zl, part_of(two, n2, h)], on_y, pairs[5]),
        )
        self.third = (
            Scatter(copies, lambda c, h: sums.at[y, c, part_of(mine, quarter, h)], on_z, pairs[6]),
            Scatter(copies, lambda c, h: sums.at[y, zl, part_of(one + rest * c, rest, h)], on_x, pairs[7]),
        )

    def cross(self, q):
        core = self.at[3]
        self.crossed.append(self.copies.start(self.grads.at[q, :, 1 - core], self.lands.at[q], self.sibling))

    def add_cores(self):
        core = self.at[3]
        for q in range(4):
            self.crossed[q].wait_recv()
            total = self.grads[q, :, core].astype(F32) + self.lands[q].astype(F32)
            self.sums[q] = total.astype(BF)

    def send_far(self):
        x, y, zl, _ = self.at
        cut = self.cut
        self.own[0 : cut.quarter] = self.sums[y, zl, pl.ds(cut.quarter * x, cut.quarter)]
        self.own[cut.quarter : cut.own] = self.sums[y, zl, pl.ds(cut.from1 + cut.rest * x, cut.rest)]
        self.far_copy = self.copies.start(self.own, self.far, self.z_far)

    def send_full(self):
        x = self.at[0]
        self.far_copy.wait_recv()
        self.full[x] = (self.own[...].astype(F32) + self.far[...].astype(F32)).astype(BF)
        mine = self.full.at[x]
        self.full_copies = [self.copies.start(mine, mine, other) for other in self.x_others]

    def wait_full(self):
        for copy in self.full_copies:
            copy.wait_recv()

    def tile(self, number):
        return self.full[self.cut.place(number)].astype(F32) * (1.0 / 256)


def kernel(
    img, wd, wc, ws, ag, sg,
    act_out, short_out, down_out, conv_out, skip_out,
    ga, gb, grad_a, grad_b, sib_a, sib_b, sum_a, sum_b,
    own_a, own_b, far_a, far_b, full_a, full_b,
    spread, padded_img, taps, cols_img, cols_first,
    send, recv, *slots,
):
    rep, shard = lax.axis_index("rep"), lax.axis_index("fsdp")
    x, y, zl, core = rep % 4, shard // 8, (shard // 2) % 4, shard % 2
    z = (rep // 4) * 4 + zl

    def device(x, y, z, core):
        return ((z // 4) * 4 + x, (y * 4 + z % 4) * 2 + core)

    sibling = device(x, y, z, 1 - core)
    x_others = [device((x + d) % 4, y, z, core) for d in (1, 2, 3)]
    y_next, y_prev = device(x, (y + 1) % 4, z, core), device(x, (y + 3) % 4, z, core)
    z_next, z_prev = device(x, y, (z + 1) % 8, core), device(x, y, (z + 7) % 8, core)
    z_far = device(x, y, (z + 4) % 8, core)
    at = (x, y, zl, core)
    rings = ((x, x_others[0], x_others[2]), (y, y_next, y_prev), (zl, z_next, z_prev))

    def place_shard(buf, values, lane_tile, per_lane, lanes):
        low = lane_tile * 128
        base = per_lane * lane_tile
        if lanes < 128:
            for row in range(ROW_TILES):
                buf[y, zl, core, base + row] = jnp.zeros((16, 128), BF)
            for row in range(ROW_TILES):
                high = min(SHARD, 16 * row + 16)
                buf[y, zl, core, base + row, 0 : high - 16 * row, 0:lanes] = values[16 * row : high, low : low + lanes]
        else:
            full = values[0:80, low : low + 128].reshape(5, 16, 128)
            buf[y, zl, core, base : base + 5] = full
            buf[y, zl, core, base + 5] = jnp.zeros((16, 128), BF)
            buf[y, zl, core, base + 5, 0:10] = values[80:SHARD, low : low + 128]

    for tile in range(3):
        place_shard(ga, wd, tile, 6, min(128, C0 - 128 * tile))
    for tile in range(5):
        place_shard(gb, wc, tile, 7, 128)
        gb[y, zl, core, 7 * tile + 6] = jnp.zeros((16, 128), BF)
        gb[y, zl, core, 7 * tile + 6, 0:SKIP] = ws[:, 128 * tile : 128 * tile + 128]

    barrier = pltpu.get_barrier_semaphore()
    greeted = [sibling, y_next, y_prev, z_next, z_prev, z_far] + x_others
    for other in greeted:
        pl.semaphore_signal(barrier, inc=1, device_id=other, device_id_type=MESH)
    pl.semaphore_wait(barrier, len(greeted))

    copies = Copies(send, recv)
    wa = Weights(copies, ga, TILES_A, at, rings, sibling)
    wb = Weights(copies, gb, TILES_B, at, rings, sibling)

    each("start", *wa.first)
    each("start", *wb.first)

    for number, (tile, tap) in enumerate(PAIRS):
        spread[number] = spread_matrix(tile, tap)
    padded_img[...] = jnp.zeros((512, LANES0), BF)
    padded_img[:, 0:C0] = img[...]

    each("forward", *wa.first)
    each("finish", *wa.first)
    each("start", *wa.second)
    each("forward", *wb.first)
    each("finish", *wb.first)
    each("start", *wb.second)
    wa.share(wa.second[1:], 0)
    wb.share(wb.second[1:], 0)

    for tap in range(9):
        taps[tap] = dot(shift_down(tap), padded_img[...]).astype(BF)

    def columns(out):
        for tile in range(COLS // TILE):
            total = None
            for number, (tile_of, tap) in enumerate(PAIRS):
                if tile_of == tile:
                    term = dot(taps[tap], spread[number])
                    total = term if total is None else total + term
            out[:, tile * TILE : (tile + 1) * TILE] = total.astype(BF)

    each("forward", *wa.second)
    wa.share(wa.second[1:], 1, 3)
    each("finish", *wa.second)
    wa.third.start()
    wa.share(wa.second[1:], 2)
    wa.share([wa.third], 0)
    each("forward", *wb.second)
    wb.share(wb.second[1:], 1, 3)

    columns(cols_img)

    wa.third.forward()
    wa.share([wa.third], 1, 3)
    each("finish", *wb.second)
    wb.third.start()
    wb.share(wb.second[1:], 2)
    wb.share([wb.third], 0)
    wa.third.finish()
    wa.share([wa.third], 2)
    wa.wait_shared()

    def chunk_of(q):
        return slice(q * CHUNK, (q + 1) * CHUNK)

    def rows_of(buf, q, lane_tiles, per_lane):
        parts = [
            buf[q, :, :, per_lane * tile : per_lane * tile + ROW_TILES].reshape(CHUNK, 128)
            for tile in range(lane_tiles)
        ]
        return jnp.concatenate(parts, axis=1)

    def down_rows(q):
        return rows_of(ga, q, 3, 6)

    def conv_rows(q):
        return rows_of(gb, q, 5, 7)

    reduced = sum(dot(cols_img[:, chunk_of(q)], down_rows(q)) for q in range(4)).astype(BF)
    same0 = group_matrix(LANES0, group10)
    normed0, scale0 = normalise(reduced.astype(F32), same0, CELLS * (C0 // 32))
    first = silu(normed0).astype(BF)
    for tap in range(9):
        taps[tap] = dot(shift_conv(tap), first).astype(BF)
    wb.third.forward()
    wb.share([wb.third], 1, 3)
    columns(cols_first)
    skip_spread = skip_matrix()
    reduced_cols = dot(reduced, skip_spread).astype(BF)
    grad_skip = dot_tn(reduced_cols, sg[...]).astype(BF)
    for tile in range(5):
        grad_b[:, :, :, 7 * tile + 6] = grad_skip[:, 128 * tile : 128 * tile + 128].reshape(4, 4, 2, 16, 128)
    grad_b[:, :, :, 35] = jnp.zeros((4, 4, 2, 16, 128), BF)
    grad_a[:, :, :, 18:20] = jnp.zeros((4, 4, 2, 2, 16, 128), BF)

    wb.third.finish()
    wb.share([wb.third], 2)
    wb.wait_shared()

    hidden = sum(dot(cols_first[:, chunk_of(q)], conv_rows(q)) for q in range(4)).astype(BF)
    same1 = group_matrix(C1, group20)
    normed1, scale1 = normalise(hidden.astype(F32), same1, CELLS * (C1 // 32))
    act_out[...] = silu(normed1).astype(BF)
    d_hidden = normalise_back(ag[...].astype(F32), normed1, scale1, same1, CELLS * (C1 // 32)).astype(BF)

    devices = (sibling, z_far, x_others)
    back_a = Gradients(copies, grad_a, sib_a, sum_a, slots[:16], (own_a, far_a, full_a), TILES_A, at, rings, devices)
    back_b = Gradients(copies, grad_b, sib_b, sum_b, slots[16:], (own_b, far_b, full_b), TILES_B, at, rings, devices)

    for q in range(4):
        part = dot_tn(cols_first[:, chunk_of(q)], d_hidden).astype(BF)
        for tile in range(5):
            grad_b[q, :, :, 7 * tile : 7 * tile + 6] = part[:, 128 * tile : 128 * tile + 128].reshape(4, 2, 6, 16, 128)
        back_b.cross(q)

    for q in range(4):
        cols_first[:, chunk_of(q)] = dot_nt(d_hidden, conv_rows(q)).astype(BF)

    back_b.add_cores()
    each("start", *back_b.first)

    d_first = jnp.zeros((CELLS, LANES0), F32)
    for tap in range(9):
        part = None
        for number, (tile, tap_of) in enumerate(PAIRS):
            if tap_of == tap:
                term = dot_nt(cols_first[:, tile * TILE : (tile + 1) * TILE], spread[number])
                part = term if part is None else part + term
        d_first = d_first + dot(shift_conv(8 - tap), part.astype(BF))

    skip_rows = jnp.concatenate([gb[:, :, :, 7 * tile + 6].reshape(512, 128) for tile in range(5)], axis=1)
    short_out[...] = dot(reduced_cols, skip_rows).astype(BF)
    d_skip = dot_nt(dot_nt(sg[...], skip_rows).astype(BF), skip_spread)
    d_norm = normalise_back(
        d_first.astype(BF).astype(F32), normed0, scale0, same0, CELLS * (C0 // 32)
    )
    d_reduced = (d_norm + d_skip).astype(BF)

    for q in range(4):
        part = dot_tn(cols_img[:, chunk_of(q)], d_reduced).astype(BF)
        for tile in range(3):
            grad_a[q, :, :, 6 * tile : 6 * tile + 6] = part[:, 128 * tile : 128 * tile + 128].reshape(4, 2, 6, 16, 128)
        back_a.cross(q)

    each("middle", *back_b.first)
    back_a.add_cores()
    each("start", *back_a.first)
    each("finish", *back_b.first)
    each("start", *back_b.second)
    each("middle", *back_a.first)
    each("middle", *back_b.second)
    each("finish", *back_b.second)
    each("start", *back_b.third)
    each("finish", *back_a.first)
    each("start", *back_a.second)
    each("middle", *back_b.third)
    each("middle", *back_a.second)
    each("finish", *back_b.third)
    back_b.send_far()
    each("finish", *back_a.second)
    each("start", *back_a.third)
    each("middle", *back_a.third)
    back_b.send_full()
    each("finish", *back_a.third)
    back_a.send_far()
    back_b.wait_full()
    for tile in range(5):
        lanes = slice(tile * 128, (tile + 1) * 128)
        for row in range(ROW_TILES):
            high = min(SHARD, 16 * row + 16)
            conv_out[16 * row : high, lanes] = back_b.tile(7 * tile + row)[0 : high - 16 * row]
        skip_out[:, lanes] = back_b.tile(7 * tile + 6)[0:SKIP]
    back_a.send_full()
    back_a.wait_full()
    for tile in range(3):
        wide = min(C0 - tile * 128, 128)
        for row in range(ROW_TILES):
            high = min(SHARD, 16 * row + 16)
            values = back_a.tile(6 * tile + row)[0 : high - 16 * row, 0:wide]
            down_out[16 * row : high, tile * 128 : tile * 128 + wide] = values

    for copy in copies.started:
        copy.wait_send()


def vmem(*shape):
    return pltpu.VMEM(shape, BF)


def tiles(*shape):
    return vmem(*shape, 16, 128)


def body(images, w_down, w_conv, w_skip, act_grad, short_grad):
    picture = images.reshape(512, C0)
    act_cot = act_grad.reshape(CELLS, C1)
    short_cot = short_grad.reshape(CELLS, C1)
    a, b = TILES_A.slots, TILES_B.slots
    slots = [tiles(3, *shape) for cut in (TILES_A, TILES_B) for pair in scatter_slots(cut) for shape in pair]

    outs = pl.pallas_call(
        kernel,
        out_shape=(
            jax.ShapeDtypeStruct((CELLS, C1), BF),
            jax.ShapeDtypeStruct((CELLS, C1), BF),
            jax.ShapeDtypeStruct((SHARD, C0), F32),
            jax.ShapeDtypeStruct((SHARD, C1), F32),
            jax.ShapeDtypeStruct((SKIP, C1), F32),
        ),
        in_specs=[pl.BlockSpec(memory_space=pltpu.VMEM)] * 6,
        out_specs=tuple([pl.BlockSpec(memory_space=pltpu.VMEM)] * 5),
        scratch_shapes=[
            tiles(4, 4, 2, a),
            tiles(4, 4, 2, b),
            tiles(4, 4, 2, a),
            tiles(4, 4, 2, b),
            tiles(4, 4, a),
            tiles(4, 4, b),
            tiles(4, 4, a),
            tiles(4, 4, b),
            tiles(TILES_A.own),
            tiles(TILES_B.own),
            tiles(TILES_A.own),
            tiles(TILES_B.own),
            tiles(4, TILES_A.own),
            tiles(4, TILES_B.own),
            vmem(len(PAIRS), LANES0, TILE),
            vmem(512, LANES0),
            vmem(9, CELLS, LANES0),
            vmem(CELLS, COLS),
            vmem(CELLS, COLS),
            pltpu.SemaphoreType.DMA((SEMS,)),
            pltpu.SemaphoreType.DMA((SEMS,)),
            *slots,
        ],
        compiler_params=pltpu.CompilerParams(
            collective_id=0, has_side_effects=True, vmem_limit_bytes=56 * 1024 * 1024
        ),
    )(picture, w_down, w_conv, w_skip, act_cot, short_cot)
    activated, shortcut, down, conv, skip = outs
    return (
        activated.reshape(act_grad.shape),
        shortcut.reshape(short_grad.shape),
        down,
        conv,
        skip,
    )


def solution(mesh):
    cells = P(("rep", "fsdp"), None, None, None)
    rows = P("fsdp", None)
    return jax.shard_map(
        body,
        mesh=mesh,
        in_specs=(cells, rows, rows, rows, cells, cells),
        out_specs=(cells, cells, rows, rows, rows),
        check_vma=False,
    )
```

```python
import jax
import jax.numpy as jnp
from jax import lax
from jax.experimental import pallas as pl
from jax.experimental.pallas import tpu as pltpu
from jax.sharding import PartitionSpec as P

MESH = pl.DeviceIdType.MESH
BF = jnp.bfloat16
F32 = jnp.float32

C0, C1 = 320, 640
LANES0 = 384
SHARD = 90
PAD = 96
SKIP, SKIP_PAD = 10, 16
ROW_TILES = PAD // 16
CELLS = 128
TILE = 256
COLS = 32 * PAD
CHUNK = 8 * PAD
SEMS = 240
EPS = 1e-5


def source_of(col):
    shard, place = divmod(col, PAD)
    return SHARD * shard + place if place < SHARD else -1


def tile_taps():
    pairs = []
    for tile in range(COLS // TILE):
        cols = [source_of(c) for c in range(tile * TILE, (tile + 1) * TILE)]
        for tap in sorted({s // C0 for s in cols if s >= 0}):
            pairs.append((tile, tap))
    return pairs


PAIRS = tile_taps()


def iota(shape, axis):
    return lax.broadcasted_iota(jnp.int32, shape, axis)


def ones_where(mask):
    return jnp.where(mask, 1.0, 0.0).astype(BF)


def spread_matrix(tile, tap):
    lane = iota((1, TILE), 1) + tile * TILE
    shard = jnp.full((1, TILE), tile * TILE // PAD, jnp.int32)
    for edge in range(PAD, COLS, PAD):
        if tile * TILE < edge < (tile + 1) * TILE:
            shard = shard + jnp.where(lane >= edge, 1, 0)
    place = lane - PAD * shard
    channel = lane - (PAD - SHARD) * shard - C0 * tap
    good = (place < SHARD) & (channel >= 0) & (channel < C0)
    channel = jnp.where(good, channel, -1)
    return ones_where(iota((LANES0, TILE), 0) == channel)


def skip_matrix():
    lane = iota((1, 32 * SKIP_PAD), 1)
    shard = lane >> 4
    place = lane - SKIP_PAD * shard
    channel = jnp.where(place < SKIP, SKIP * shard + place, -1)
    return ones_where(iota((LANES0, 32 * SKIP_PAD), 0) == channel)


def shift_down(tap):
    kh, kw = divmod(tap, 3)
    cell = iota((CELLS, 1), 0)
    row, col = 2 * (cell >> 4) + kh - 1, 2 * (cell & 15) + kw - 1
    index = jnp.where((row >= 0) & (col >= 0), row * 32 + col, -1)
    return ones_where(iota((CELLS, 512), 1) == index)


def shift_conv(tap):
    kh, kw = divmod(tap, 3)
    cell = iota((CELLS, 1), 0)
    row, col = (cell >> 4) + kh - 1, (cell & 15) + kw - 1
    good = (row >= 0) & (row < 8) & (col >= 0) & (col < 16)
    index = jnp.where(good, row * 16 + col, -1)
    return ones_where(iota((CELLS, CELLS), 1) == index)


def dot(a, b):
    return lax.dot_general(a, b, (((1,), (0,)), ((), ())), preferred_element_type=F32)


def dot_nt(a, b):
    return lax.dot_general(a, b, (((1,), (1,)), ((), ())), preferred_element_type=F32)


def dot_tn(a, b):
    return lax.dot_general(a, b, (((0,), (0,)), ((), ())), preferred_element_type=F32)


def group_matrix(width, group_of):
    return ones_where(group_of(iota((width, width), 0)) == group_of(iota((width, width), 1)))


def group10(c):
    return (c * 6554) >> 16


def group20(c):
    return (c * 3277) >> 16


def group_sums(vectors, same):
    width = same.shape[0]
    row = iota((8, width), 0)
    stacked = jnp.zeros((8, width), F32)
    for number, vector in enumerate(vectors):
        rest = vector
        for term in range(3):
            part = rest.astype(BF).astype(F32)
            rest = rest - part
            stacked = jnp.where(row == 4 * number + term, part, stacked)
    sums = dot(stacked.astype(BF), same)
    return [jnp.sum(sums[4 * n : 4 * n + 4], axis=0, keepdims=True) for n in range(len(vectors))]


def normalise(values, same, count):
    (total,) = group_sums([jnp.sum(values, axis=0, keepdims=True)], same)
    centred = values - total * (1.0 / count)
    (square,) = group_sums([jnp.sum(centred * centred, axis=0, keepdims=True)], same)
    scale = lax.rsqrt(square * (1.0 / count) + EPS)
    return centred * scale, scale


def normalise_back(cotangent, normed, scale, same, count):
    sig = 1.0 / (1.0 + jnp.exp(-normed))
    slope = cotangent * (sig * (1.0 + normed * (1.0 - sig)))
    first, second = group_sums(
        [jnp.sum(slope, axis=0, keepdims=True), jnp.sum(slope * normed, axis=0, keepdims=True)], same
    )
    return scale * (slope - first * (1.0 / count) - normed * (second * (1.0 / count)))


def silu(normed):
    return normed / (1.0 + jnp.exp(-normed))


class Tiles:
    def __init__(self, count, slots):
        first = (count + 1) // 2
        self.routes = ((0, first), (first, count - first))
        self.slots, self.quarter = slots, slots // 4


TILES_A = Tiles(18, 20)
TILES_B = Tiles(35, 36)


class Copies:
    def __init__(self, send, recv):
        self.send, self.recv, self.started = send, recv, []

    def start(self, src, dst, device):
        number = len(self.started)
        copy = pltpu.make_async_remote_copy(
            src_ref=src,
            dst_ref=dst,
            send_sem=self.send.at[number],
            recv_sem=self.recv.at[number],
            device_id=device,
            device_id_type=MESH,
        )
        copy.start()
        self.started.append(copy)
        return copy


class Spread:
    def __init__(self, copies, piece, row, light, heavy, sibling):
        self.copies, self.piece, self.row, self.sibling = copies, piece, row, sibling
        self.light, self.heavy = light, heavy
        self.to = {}
        self.shared = []

    def send(self, i, j, device, name):
        ref = self.piece(i, j)
        self.to[name] = self.copies.start(ref, ref, device)

    def wait(self, *names):
        for name in names:
            self.to[name].wait_recv()

    def both(self, i):
        self.send(i, 0, self.heavy[0], ("after", i))
        self.send(i, 0, self.heavy[1], ("before", i))

    def s0(self):
        for d in (2, 1, 3):
            self.send(0, 0, self.light[d - 1], ("light", d))
        self.both(0)

    def s1(self):
        for d in (1, 3, 2):
            self.wait(("light", d))
            self.both(4 - d)

    def s2(self):
        self.wait(("after", 0))
        self.send(0, 3, self.heavy[0], ("far", 0))

    def s4(self):
        for i in (3, 1):
            self.wait(("before", i))
            self.send(i, 1, self.heavy[1], ("far", i))

    def s5(self):
        self.wait(("after", 2))
        self.send(2, 3, self.heavy[0], ("far", 2))
        self.wait(("after", 1), ("after", 3), ("before", 0), ("before", 2))

    def s6(self):
        self.wait(("far", 0), ("far", 1), ("far", 2), ("far", 3))

    def share(self, *offsets):
        for offset in offsets:
            ref = self.row(offset)
            self.shared.append(self.copies.start(ref, ref, self.sibling))

    def end(self):
        for copy in self.shared:
            copy.wait_recv()


def add_into(ref, *others):
    total = ref[...].astype(F32)
    for other in others:
        total = total + other[...].astype(F32)
    ref[...] = total.astype(BF)


class Collect:
    def __init__(self, copies, piece, light, heavy, lands, ends):
        self.copies, self.piece = copies, piece
        self.light, self.heavy = light, heavy
        self.lands, self.ends = lands, ends
        self.to = {}

    def send(self, i, j, land, device, name):
        self.to[name] = self.copies.start(self.piece(i, j), land, device)

    def r0(self):
        after, before = self.heavy
        for i, device in ((2, after), (1, before), (3, before), (0, after)):
            self.send(i, 2, self.lands.at[i], device, ("far", i))
        for i, j, device in ((2, 3, before), (1, 1, after), (3, 1, after), (0, 3, before)):
            self.send(i, j, self.lands.at[4 + i], device, ("near", i))

    def r1(self):
        after, before = self.heavy
        for i, j, device in ((2, 1, after), (1, 3, before), (3, 3, before), (0, 1, after)):
            self.to["far", i].wait_recv()
            add_into(self.piece(i, j), self.lands.at[i])
            self.send(i, j, self.lands.at[8 + i], device, ("next", i))

    def r2(self):
        for i in (2, 1, 3, 0):
            self.to["near", i].wait_recv()
            self.to["next", i].wait_recv()
            add_into(self.piece(i, 0), self.lands.at[4 + i], self.lands.at[8 + i])
            if i > 0:
                self.send(i, 0, self.ends.at[i - 1], self.light[i - 1], ("light", i))

    def r3(self):
        for i in (2, 1, 3):
            self.to["light", i].wait_recv()
        add_into(self.piece(0, 0), *(self.ends.at[slot] for slot in range(3)))


def each(method, *routes, args=()):
    for route in routes:
        getattr(route, method)(*args)


def pieces(buf, cut, at, tail):
    _, y, zl, _ = at
    one, two = (pl.ds(*route) for route in cut.routes)

    def piece0(i, j):
        return buf.at[((y + j) % 4, (zl + i) % 4, *tail, one)]

    def piece1(i, j):
        return buf.at[((y + i) % 4, (zl + j) % 4, *tail, two)]

    def row0(j):
        return buf.at[((y + j) % 4, pl.ds(0, 4), *tail, one)]

    def row1(j):
        return buf.at[(pl.ds(0, 4), (zl + j) % 4, *tail, two)]

    return (piece0, row0), (piece1, row1)


def spreads(copies, buf, cut, at, rings, sibling):
    (y_all, y_ring), (z_all, z_ring) = rings
    (piece0, row0), (piece1, row1) = pieces(buf, cut, at, (at[3],))
    return (
        Spread(copies, piece0, row0, z_all, y_ring, sibling),
        Spread(copies, piece1, row1, y_all, z_ring, sibling),
    )


class Gradients:
    def __init__(self, copies, grads, lands, sums, slots, cut, at, rings, devices):
        self.copies, self.grads, self.lands, self.sums, self.cut, self.at = copies, grads, lands, sums, cut, at
        (y_all, y_ring), (z_all, z_ring) = rings
        land0, end0, land1, end1, self.from_x, self.own, self.far, self.full = slots
        self.sibling, self.z_far, self.x_others = devices
        self.crossed = []
        (piece0, _), (piece1, _) = pieces(sums, cut, at, ())
        self.routes = (
            Collect(copies, piece0, z_all, y_ring, land0, end0),
            Collect(copies, piece1, y_all, z_ring, land1, end1),
        )

    def cross(self, q):
        core = self.at[3]
        self.crossed.append(self.copies.start(self.grads.at[q, :, 1 - core], self.lands.at[q], self.sibling))

    def add_cores(self):
        core = self.at[3]
        for q in range(4):
            self.crossed[q].wait_recv()
            total = self.grads[q, :, core].astype(F32) + self.lands[q].astype(F32)
            self.sums[q] = total.astype(BF)

    def quarter(self, c):
        _, y, zl, _ = self.at
        return self.sums.at[y, zl, pl.ds(self.cut.quarter * (c % 4), self.cut.quarter)]

    def send_x(self):
        x = self.at[0]
        self.x_copies = [
            self.copies.start(self.quarter(x + d), self.from_x.at[d - 1], self.x_others[d - 1]) for d in (1, 2, 3)
        ]

    def send_far(self):
        for copy in self.x_copies:
            copy.wait_recv()
        total = self.quarter(self.at[0])[...].astype(F32)
        for slot in range(3):
            total = total + self.from_x[slot].astype(F32)
        self.own[...] = total.astype(BF)
        self.far_copy = self.copies.start(self.own, self.far, self.z_far)

    def send_full(self):
        x = self.at[0]
        self.far_copy.wait_recv()
        self.full[x] = (self.own[...].astype(F32) + self.far[...].astype(F32)).astype(BF)
        mine = self.full.at[x]
        self.full_copies = [self.copies.start(mine, mine, other) for other in self.x_others]

    def wait_full(self):
        for copy in self.full_copies:
            copy.wait_recv()

    def tile(self, number):
        return self.full[divmod(number, self.cut.quarter)].astype(F32) * (1.0 / 256)


def kernel(
    img_in, wd_in, wc_in, ws_in, ag_in, sg_in,
    act_hbm, short_hbm, down_out, conv_out, skip_out,
    img, wd, wc, ws, ag, sg, act_out, short_out, local,
    ga, gb, grad_a, grad_b, sib_a, sib_b, sum_a, sum_b,
    spread, padded_img, taps, cols_img, cols_first,
    send, recv, *slots,
):
    rep, shard = lax.axis_index("rep"), lax.axis_index("fsdp")
    x, y, zl, core = rep % 4, shard // 8, (shard // 2) % 4, shard % 2
    z = (rep // 4) * 4 + zl

    def device(x, y, z, core):
        return ((z // 4) * 4 + x, (y * 4 + z % 4) * 2 + core)

    sibling = device(x, y, z, 1 - core)
    x_others = [device((x + d) % 4, y, z, core) for d in (1, 2, 3)]
    y_all = [device(x, (y + d) % 4, z, core) for d in (1, 2, 3)]
    z_all = [device(x, y, (z + d) % 8, core) for d in (1, 2 + 4 * core, 7)]
    z_two_back = device(x, y, (z + 6 + 4 * core) % 8, core)
    z_far = device(x, y, (z + 4) % 8, core)
    at = (x, y, zl, core)
    rings = ((y_all, (y_all[0], y_all[2])), (z_all, (z_all[0], z_all[2])))

    barrier = pltpu.get_barrier_semaphore()
    greeted = [sibling, z_far, z_two_back] + x_others + y_all + z_all
    for other in greeted:
        pl.semaphore_signal(barrier, inc=1, device_id=other, device_id_type=MESH)
    loads = [
        pltpu.make_async_copy(src, dst, local.at[number])
        for number, (src, dst) in enumerate(
            ((wd_in, wd), (wc_in, wc), (ws_in, ws), (img_in, img), (ag_in, ag), (sg_in, sg))
        )
    ]
    for load in loads:
        load.start()
    for load in loads[:3]:
        load.wait()

    def place_shard(buf, values, lane_tile, per_lane, lanes):
        low = lane_tile * 128
        base = per_lane * lane_tile
        if lanes < 128:
            for row in range(ROW_TILES):
                buf[y, zl, core, base + row] = jnp.zeros((16, 128), BF)
            for row in range(ROW_TILES):
                high = min(SHARD, 16 * row + 16)
                buf[y, zl, core, base + row, 0 : high - 16 * row, 0:lanes] = values[16 * row : high, low : low + lanes]
        else:
            full = values[0:80, low : low + 128].reshape(5, 16, 128)
            buf[y, zl, core, base : base + 5] = full
            buf[y, zl, core, base + 5] = jnp.zeros((16, 128), BF)
            buf[y, zl, core, base + 5, 0:10] = values[80:SHARD, low : low + 128]

    for tile in range(3):
        place_shard(ga, wd, tile, 6, min(128, C0 - 128 * tile))
    for tile in range(5):
        place_shard(gb, wc, tile, 7, 128)
        gb[y, zl, core, 7 * tile + 6] = jnp.zeros((16, 128), BF)
        gb[y, zl, core, 7 * tile + 6, 0:SKIP] = ws[:, 128 * tile : 128 * tile + 128]

    pl.semaphore_wait(barrier, len(greeted))

    copies = Copies(send, recv)
    wa = spreads(copies, ga, TILES_A, at, rings, sibling)
    wb = spreads(copies, gb, TILES_B, at, rings, sibling)

    each("s0", *wa)
    each("s0", *wb)

    for number, (tile, tap) in enumerate(PAIRS):
        spread[number] = spread_matrix(tile, tap)
    for load in loads[3:]:
        load.wait()
    padded_img[...] = jnp.zeros((512, LANES0), BF)
    padded_img[:, 0:C0] = img[...]

    each("s1", *wa)
    each("s1", *wb)
    each("s2", *wa)
    each("share", *wa, args=(0,))
    each("s2", *wb)
    each("share", *wb, args=(0,))

    for tap in range(9):
        taps[tap] = dot(shift_down(tap), padded_img[...]).astype(BF)

    def columns(out):
        for tile in range(COLS // TILE):
            total = None
            for number, (tile_of, tap) in enumerate(PAIRS):
                if tile_of == tile:
                    term = dot(taps[tap], spread[number])
                    total = term if total is None else total + term
            out[:, tile * TILE : (tile + 1) * TILE] = total.astype(BF)

    each("s4", *wa)
    each("s5", *wa)
    each("share", *wa, args=(1, 3))
    each("s4", *wb)
    columns(cols_img)
    each("s6", *wa)
    each("share", *wa, args=(2,))
    each("s5", *wb)
    each("share", *wb, args=(1, 3))
    each("end", *wa)

    def chunk_of(q):
        return slice(q * CHUNK, (q + 1) * CHUNK)

    def rows_of(buf, q, lane_tiles, per_lane):
        parts = [
            buf[q, :, :, per_lane * tile : per_lane * tile + ROW_TILES].reshape(CHUNK, 128)
            for tile in range(lane_tiles)
        ]
        return jnp.concatenate(parts, axis=1)

    def down_rows(q):
        return rows_of(ga, q, 3, 6)

    def conv_rows(q):
        return rows_of(gb, q, 5, 7)

    reduced = sum(dot(cols_img[:, chunk_of(q)], down_rows(q)) for q in range(4)).astype(BF)
    same0 = group_matrix(LANES0, group10)
    normed0, scale0 = normalise(reduced.astype(F32), same0, CELLS * (C0 // 32))
    first = silu(normed0).astype(BF)
    for tap in range(9):
        taps[tap] = dot(shift_conv(tap), first).astype(BF)
    columns(cols_first)
    skip_spread = skip_matrix()
    reduced_cols = dot(reduced, skip_spread).astype(BF)
    grad_skip = dot_tn(reduced_cols, sg[...]).astype(BF)
    for tile in range(5):
        grad_b[:, :, :, 7 * tile + 6] = grad_skip[:, 128 * tile : 128 * tile + 128].reshape(4, 4, 2, 16, 128)
    grad_b[:, :, :, 35] = jnp.zeros((4, 4, 2, 16, 128), BF)
    grad_a[:, :, :, 18:20] = jnp.zeros((4, 4, 2, 2, 16, 128), BF)

    each("s6", *wb)
    each("share", *wb, args=(2,))
    each("end", *wb)

    hidden = sum(dot(cols_first[:, chunk_of(q)], conv_rows(q)) for q in range(4)).astype(BF)
    same1 = group_matrix(C1, group20)
    normed1, scale1 = normalise(hidden.astype(F32), same1, CELLS * (C1 // 32))
    act_out[...] = silu(normed1).astype(BF)
    act_store = pltpu.make_async_copy(act_out, act_hbm, local.at[6])
    act_store.start()
    d_hidden = normalise_back(ag[...].astype(F32), normed1, scale1, same1, CELLS * (C1 // 32)).astype(BF)

    devices = (sibling, z_far, x_others)
    back_a = Gradients(copies, grad_a, sib_a, sum_a, slots[:8], TILES_A, at, rings, devices)
    back_b = Gradients(copies, grad_b, sib_b, sum_b, slots[8:], TILES_B, at, rings, devices)

    for q in range(4):
        part = dot_tn(cols_first[:, chunk_of(q)], d_hidden).astype(BF)
        for tile in range(5):
            grad_b[q, :, :, 7 * tile : 7 * tile + 6] = part[:, 128 * tile : 128 * tile + 128].reshape(4, 2, 6, 16, 128)
        back_b.cross(q)

    for q in range(4):
        cols_first[:, chunk_of(q)] = dot_nt(d_hidden, conv_rows(q)).astype(BF)

    back_b.add_cores()
    each("r0", *back_b.routes)

    d_first = jnp.zeros((CELLS, LANES0), F32)
    for tap in range(9):
        part = None
        for number, (tile, tap_of) in enumerate(PAIRS):
            if tap_of == tap:
                term = dot_nt(cols_first[:, tile * TILE : (tile + 1) * TILE], spread[number])
                part = term if part is None else part + term
        d_first = d_first + dot(shift_conv(8 - tap), part.astype(BF))

    skip_rows = jnp.concatenate([gb[:, :, :, 7 * tile + 6].reshape(512, 128) for tile in range(5)], axis=1)
    short_out[...] = dot(reduced_cols, skip_rows).astype(BF)
    short_store = pltpu.make_async_copy(short_out, short_hbm, local.at[7])
    short_store.start()
    d_skip = dot_nt(dot_nt(sg[...], skip_rows).astype(BF), skip_spread)
    d_norm = normalise_back(
        d_first.astype(BF).astype(F32), normed0, scale0, same0, CELLS * (C0 // 32)
    )
    d_reduced = (d_norm + d_skip).astype(BF)

    for q in range(4):
        part = dot_tn(cols_img[:, chunk_of(q)], d_reduced).astype(BF)
        for tile in range(3):
            grad_a[q, :, :, 6 * tile : 6 * tile + 6] = part[:, 128 * tile : 128 * tile + 128].reshape(4, 2, 6, 16, 128)
        back_a.cross(q)

    each("r1", *back_b.routes)
    back_a.add_cores()
    each("r0", *back_a.routes)
    each("r2", *back_b.routes)
    each("r1", *back_a.routes)
    each("r3", *back_b.routes)
    back_b.send_x()
    each("r2", *back_a.routes)
    back_b.send_far()
    each("r3", *back_a.routes)
    back_a.send_x()
    back_b.send_full()
    back_a.send_far()
    back_b.wait_full()
    for tile in range(5):
        lanes = slice(tile * 128, (tile + 1) * 128)
        for row in range(ROW_TILES):
            high = min(SHARD, 16 * row + 16)
            conv_out[16 * row : high, lanes] = back_b.tile(7 * tile + row)[0 : high - 16 * row]
        skip_out[:, lanes] = back_b.tile(7 * tile + 6)[0:SKIP]
    back_a.send_full()
    back_a.wait_full()
    for tile in range(3):
        wide = min(C0 - tile * 128, 128)
        for row in range(ROW_TILES):
            high = min(SHARD, 16 * row + 16)
            values = back_a.tile(6 * tile + row)[0 : high - 16 * row, 0:wide]
            down_out[16 * row : high, tile * 128 : tile * 128 + wide] = values

    act_store.wait()
    short_store.wait()
    for copy in copies.started:
        copy.wait_send()


def vmem(*shape):
    return pltpu.VMEM(shape, BF)


def tiles(*shape):
    return vmem(*shape, 16, 128)


def body(images, w_down, w_conv, w_skip, act_grad, short_grad):
    picture = images.reshape(512, C0)
    act_cot = act_grad.reshape(CELLS, C1)
    short_cot = short_grad.reshape(CELLS, C1)
    a, b = TILES_A.slots, TILES_B.slots
    slots = []
    for cut in (TILES_A, TILES_B):
        for _, count in cut.routes:
            slots += [tiles(12, count), tiles(3, count)]
        slots += [tiles(3, cut.quarter), tiles(cut.quarter), tiles(cut.quarter), tiles(4, cut.quarter)]

    outs = pl.pallas_call(
        kernel,
        out_shape=(
            jax.ShapeDtypeStruct((CELLS, C1), BF),
            jax.ShapeDtypeStruct((CELLS, C1), BF),
            jax.ShapeDtypeStruct((SHARD, C0), F32),
            jax.ShapeDtypeStruct((SHARD, C1), F32),
            jax.ShapeDtypeStruct((SKIP, C1), F32),
        ),
        in_specs=[pl.BlockSpec(memory_space=pl.ANY)] * 6,
        out_specs=tuple([pl.BlockSpec(memory_space=pl.ANY)] * 2 + [pl.BlockSpec(memory_space=pltpu.VMEM)] * 3),
        scratch_shapes=[
            vmem(512, C0),
            vmem(SHARD, C0),
            vmem(SHARD, C1),
            vmem(SKIP, C1),
            *[vmem(CELLS, C1)] * 4,
            pltpu.SemaphoreType.DMA((8,)),
            tiles(4, 4, 2, a),
            tiles(4, 4, 2, b),
            tiles(4, 4, 2, a),
            tiles(4, 4, 2, b),
            tiles(4, 4, a),
            tiles(4, 4, b),
            tiles(4, 4, a),
            tiles(4, 4, b),
            vmem(len(PAIRS), LANES0, TILE),
            vmem(512, LANES0),
            vmem(9, CELLS, LANES0),
            vmem(CELLS, COLS),
            vmem(CELLS, COLS),
            pltpu.SemaphoreType.DMA((SEMS,)),
            pltpu.SemaphoreType.DMA((SEMS,)),
            *slots,
        ],
        compiler_params=pltpu.CompilerParams(
            collective_id=0, has_side_effects=True, vmem_limit_bytes=56 * 1024 * 1024
        ),
    )(picture, w_down, w_conv, w_skip, act_cot, short_cot)
    activated, shortcut, down, conv, skip = outs
    return (
        activated.reshape(act_grad.shape),
        shortcut.reshape(short_grad.shape),
        down,
        conv,
        skip,
    )


def solution(mesh):
    cells = P(("rep", "fsdp"), None, None, None)
    rows = P("fsdp", None)
    return jax.shard_map(
        body,
        mesh=mesh,
        in_specs=(cells, rows, rows, rows, cells, cells),
        out_specs=(cells, cells, rows, rows, rows),
        check_vma=False,
    )
```

```python
import jax
import jax.numpy as jnp
from jax import lax
from jax.experimental import pallas as pl
from jax.experimental.pallas import tpu as pltpu
from jax.sharding import PartitionSpec as P

MESH = pl.DeviceIdType.MESH
BF = jnp.bfloat16
F32 = jnp.float32

C0, C1 = 320, 640
LANES0 = 384
SHARD = 90
PAD = 96
SKIP, SKIP_PAD = 10, 16
ROW_TILES = PAD // 16
CELLS = 128
TILE = 256
COLS = 32 * PAD
CHUNK = 8 * PAD
SEMS = 84
EPS = 1e-5


def source_of(col):
    shard, place = divmod(col, PAD)
    return SHARD * shard + place if place < SHARD else -1


def tile_taps():
    pairs = []
    for tile in range(COLS // TILE):
        cols = [source_of(c) for c in range(tile * TILE, (tile + 1) * TILE)]
        for tap in sorted({s // C0 for s in cols if s >= 0}):
            pairs.append((tile, tap))
    return pairs


PAIRS = tile_taps()


def iota(shape, axis):
    return lax.broadcasted_iota(jnp.int32, shape, axis)


def ones_where(mask):
    return jnp.where(mask, 1.0, 0.0).astype(BF)


def spread_matrix(tile, tap):
    lane = iota((1, TILE), 1) + tile * TILE
    shard = jnp.full((1, TILE), tile * TILE // PAD, jnp.int32)
    for edge in range(PAD, COLS, PAD):
        if tile * TILE < edge < (tile + 1) * TILE:
            shard = shard + jnp.where(lane >= edge, 1, 0)
    place = lane - PAD * shard
    channel = lane - (PAD - SHARD) * shard - C0 * tap
    good = (place < SHARD) & (channel >= 0) & (channel < C0)
    channel = jnp.where(good, channel, -1)
    return ones_where(iota((LANES0, TILE), 0) == channel)


def skip_matrix():
    lane = iota((1, 32 * SKIP_PAD), 1)
    shard = lane >> 4
    place = lane - SKIP_PAD * shard
    channel = jnp.where(place < SKIP, SKIP * shard + place, -1)
    return ones_where(iota((LANES0, 32 * SKIP_PAD), 0) == channel)


def shift_down(tap):
    kh, kw = divmod(tap, 3)
    cell = iota((CELLS, 1), 0)
    row, col = 2 * (cell >> 4) + kh - 1, 2 * (cell & 15) + kw - 1
    index = jnp.where((row >= 0) & (col >= 0), row * 32 + col, -1)
    return ones_where(iota((CELLS, 512), 1) == index)


def shift_conv(tap):
    kh, kw = divmod(tap, 3)
    cell = iota((CELLS, 1), 0)
    row, col = (cell >> 4) + kh - 1, (cell & 15) + kw - 1
    good = (row >= 0) & (row < 8) & (col >= 0) & (col < 16)
    index = jnp.where(good, row * 16 + col, -1)
    return ones_where(iota((CELLS, CELLS), 1) == index)


def dot(a, b):
    return lax.dot_general(a, b, (((1,), (0,)), ((), ())), preferred_element_type=F32)


def dot_nt(a, b):
    return lax.dot_general(a, b, (((1,), (1,)), ((), ())), preferred_element_type=F32)


def dot_tn(a, b):
    return lax.dot_general(a, b, (((0,), (0,)), ((), ())), preferred_element_type=F32)


def group_matrix(width, group_of):
    return ones_where(group_of(iota((width, width), 0)) == group_of(iota((width, width), 1)))


def group10(c):
    return (c * 6554) >> 16


def group20(c):
    return (c * 3277) >> 16


def group_sums(vectors, same):
    width = same.shape[0]
    row = iota((8, width), 0)
    stacked = jnp.zeros((8, width), F32)
    for number, vector in enumerate(vectors):
        rest = vector
        for term in range(3):
            part = rest.astype(BF).astype(F32)
            rest = rest - part
            stacked = jnp.where(row == 4 * number + term, part, stacked)
    sums = dot(stacked.astype(BF), same)
    return [jnp.sum(sums[4 * n : 4 * n + 4], axis=0, keepdims=True) for n in range(len(vectors))]


def normalise(values, same, count):
    (total,) = group_sums([jnp.sum(values, axis=0, keepdims=True)], same)
    centred = values - total * (1.0 / count)
    (square,) = group_sums([jnp.sum(centred * centred, axis=0, keepdims=True)], same)
    scale = lax.rsqrt(square * (1.0 / count) + EPS)
    return centred * scale, scale


def normalise_back(cotangent, normed, scale, same, count):
    sig = 1.0 / (1.0 + jnp.exp(-normed))
    slope = cotangent * (sig * (1.0 + normed * (1.0 - sig)))
    first, second = group_sums(
        [jnp.sum(slope, axis=0, keepdims=True), jnp.sum(slope * normed, axis=0, keepdims=True)], same
    )
    return scale * (slope - first * (1.0 / count) - normed * (second * (1.0 / count)))


def silu(normed):
    return normed / (1.0 + jnp.exp(-normed))


class Tiles:
    def __init__(self, count, slots):
        first = (count + 1) // 2
        self.routes = ((0, first), (first, count - first))
        self.slots, self.quarter = slots, slots // 4


TILES_A = Tiles(18, 20)
TILES_B = Tiles(35, 36)


class Copies:
    def __init__(self, sems):
        self.sems, self.numbers = sems, {}

    def sem(self, *key):
        return self.sems.at[self.numbers.setdefault(key, len(self.numbers))]

    def start(self, src, dst, device, send, recv):
        pltpu.make_async_remote_copy(
            src_ref=src,
            dst_ref=dst,
            send_sem=self.sem("send", *send),
            recv_sem=self.sem("recv", *recv),
            device_id=device,
            device_id_type=MESH,
        ).start()

    def wait(self, way, key, ref):
        pltpu.make_async_copy(ref, ref, self.sem(way, *key)).wait()


class Spread:
    def __init__(self, copies, name, piece, row, light, heavy, sibling, other, sent):
        self.copies, self.name, self.piece, self.row, self.sibling = copies, name, piece, row, sibling
        self.light, self.heavy, self.other, self.sent = light, heavy, other, sent

    def send(self, i, j, device, recv):
        ref = self.piece(i, j)
        self.copies.start(ref, ref, device, (self.name,), (self.name, recv))

    def wait(self, recv, ref):
        self.copies.wait("recv", (self.name, recv), ref)

    def both(self, i):
        after, before = {0: ("a0", "rest"), 1: ("rest", "b"), 2: ("a2", "rest"), 3: ("rest", "b")}[i]
        self.send(i, 0, self.heavy[0], after)
        self.send(i, 0, self.heavy[1], before)

    def s0(self):
        for d in (2, 1, 3):
            self.send(0, 0, self.light[d - 1], d)
        self.both(0)

    def s1(self):
        for d in (1, 3, 2):
            self.wait(d, self.piece(4 - d, 0))
            self.both(4 - d)

    def s2(self):
        self.wait("a0", self.piece(0, 3))
        self.send(0, 3, self.heavy[0], "far")

    def s4(self):
        self.wait("b", self.sent.at[pl.ds(0, 2)])
        for i in (3, 1):
            self.send(i, 1, self.heavy[1], "far")

    def s5(self):
        self.wait("a2", self.piece(2, 3))
        self.send(2, 3, self.heavy[0], "far")
        self.wait("rest", self.sent.at[pl.ds(0, 4)])

    def s6(self):
        self.wait("far", self.row(2))

    def share(self, *offsets):
        for offset in offsets:
            ref = self.row(offset)
            self.copies.start(ref, ref, self.sibling, (self.name, "core"), (self.name, "core"))

    def end(self):
        self.copies.wait("recv", (self.name, "core"), self.other)

    def drain(self):
        self.copies.wait("send", (self.name, "core"), self.other)
        self.copies.wait("send", (self.name,), self.sent)


def add_into(ref, *others):
    total = ref[...].astype(F32)
    for other in others:
        total = total + other[...].astype(F32)
    ref[...] = total.astype(BF)


class Collect:
    def __init__(self, copies, name, piece, light, heavy, lands):
        self.copies, self.name, self.piece = copies, name, piece
        self.light, self.heavy, self.lands = light, heavy, lands

    def send(self, i, j, land, device, recv):
        self.copies.start(self.piece(i, j), self.lands.at[land], device, (self.name,), (self.name, recv))

    def wait(self, recv, start, count):
        self.copies.wait("recv", (self.name, recv), self.lands.at[pl.ds(start, count)])

    def r0(self):
        after, before = self.heavy
        for slot, (i, device) in enumerate(((2, after), (1, before), (3, before), (0, after))):
            self.send(i, 2, slot, device, ("far", slot // 2))
        for i, j, device in ((2, 3, before), (1, 1, after), (3, 1, after), (0, 3, before)):
            self.send(i, j, 8 + i, device, "near")

    def r1(self):
        after, before = self.heavy
        for slot, (i, j, device) in enumerate(((2, 1, after), (1, 3, before), (3, 3, before), (0, 1, after))):
            if slot % 2 == 0:
                self.wait(("far", slot // 2), slot, 2)
            add_into(self.piece(i, j), self.lands.at[slot])
            self.send(i, j, 4 + slot, device, ("next", slot // 2))

    def r2(self):
        self.wait("near", 8, 4)
        for slot, i in enumerate((2, 1, 3, 0)):
            if slot % 2 == 0:
                self.wait(("next", slot // 2), 4 + slot, 2)
            add_into(self.piece(i, 0), self.lands.at[8 + i], self.lands.at[4 + slot])
            if i > 0:
                self.send(i, 0, 11 + i, self.light[i - 1], "light")

    def r3(self):
        self.wait("light", 12, 3)
        add_into(self.piece(0, 0), *(self.lands.at[slot] for slot in (12, 13, 14)))

    def drain(self):
        self.copies.wait("send", (self.name,), self.lands)


def each(method, *routes, args=()):
    for route in routes:
        getattr(route, method)(*args)


def pieces(buf, cut, at, tail):
    _, y, zl, _ = at
    one, two = (pl.ds(*route) for route in cut.routes)

    def piece0(i, j):
        return buf.at[((y + j) % 4, (zl + i) % 4, *tail, one)]

    def piece1(i, j):
        return buf.at[((y + i) % 4, (zl + j) % 4, *tail, two)]

    def row0(j):
        return buf.at[((y + j) % 4, pl.ds(0, 4), *tail, one)]

    def row1(j):
        return buf.at[(pl.ds(0, 4), (zl + j) % 4, *tail, two)]

    return (piece0, row0), (piece1, row1)


def spreads(copies, name, buf, cut, at, rings, sibling, lands):
    (y_all, y_ring), (z_all, z_ring) = rings
    (piece0, row0), (piece1, row1) = pieces(buf, cut, at, (at[3],))
    other0, other1 = (buf.at[pl.ds(0, 4), pl.ds(0, 4), 1 - at[3], pl.ds(*route)] for route in cut.routes)
    return (
        Spread(copies, (name, 0), piece0, row0, z_all, y_ring, sibling, other0, lands[0]),
        Spread(copies, (name, 1), piece1, row1, y_all, z_ring, sibling, other1, lands[1]),
    )


class Gradients:
    def __init__(self, copies, name, grads, lands, sums, slots, cut, at, rings, devices):
        self.copies, self.grads, self.lands, self.sums, self.cut, self.at = copies, grads, lands, sums, cut, at
        (y_all, y_ring), (z_all, z_ring) = rings
        land0, land1, self.ends, self.full = slots
        self.sibling, self.z_far, self.x_others = devices
        self.name = name
        (piece0, _), (piece1, _) = pieces(sums, cut, at, ())
        self.routes = (
            Collect(copies, (name, 2), piece0, z_all, y_ring, land0),
            Collect(copies, (name, 3), piece1, y_all, z_ring, land1),
        )

    def cross(self, q):
        core, key = self.at[3], (self.name, "cross")
        self.copies.start(self.grads.at[q, :, 1 - core], self.lands.at[q], self.sibling, key, key)

    def add_cores(self):
        core = self.at[3]
        self.copies.wait("recv", (self.name, "cross"), self.lands)
        for q in range(4):
            total = self.grads[q, :, core].astype(F32) + self.lands[q].astype(F32)
            self.sums[q] = total.astype(BF)

    def quarter(self, c):
        _, y, zl, _ = self.at
        return self.sums.at[y, zl, pl.ds(self.cut.quarter * (c % 4), self.cut.quarter)]

    def send_x(self):
        x = self.at[0]
        for d in (1, 2, 3):
            self.copies.start(
                self.quarter(x + d), self.ends.at[d - 1], self.x_others[d - 1], (self.name,), (self.name, "x")
            )

    def send_far(self):
        self.copies.wait("recv", (self.name, "x"), self.ends.at[pl.ds(0, 3)])
        total = self.quarter(self.at[0])[...].astype(F32)
        for slot in range(3):
            total = total + self.ends[slot].astype(F32)
        self.ends[3] = total.astype(BF)
        self.copies.start(self.ends.at[3], self.ends.at[4], self.z_far, (self.name,), (self.name, "z"))

    def send_full(self):
        x = self.at[0]
        self.copies.wait("recv", (self.name, "z"), self.ends.at[4])
        self.full[x] = (self.ends[3].astype(F32) + self.ends[4].astype(F32)).astype(BF)
        mine = self.full.at[x]
        for other in self.x_others:
            self.copies.start(mine, mine, other, (self.name,), (self.name, "full"))

    def wait_full(self):
        self.copies.wait("recv", (self.name, "full"), self.ends.at[pl.ds(0, 3)])

    def drain(self):
        self.copies.wait("send", (self.name, "cross"), self.lands)
        self.copies.wait("send", (self.name,), self.ends)


def kernel(
    img_in, wd_in, wc_in, ws_in, ag_in, sg_in,
    act_hbm, short_hbm, full_a_out, full_b_out,
    img, wd, wc, ws, ag, sg, act_out, short_out, local,
    ga, gb, grad_a, grad_b, sib_a, sib_b, sum_a, sum_b,
    spread, padded_img, taps, cols_img, cols_first,
    sems, *slots,
):
    rep, shard = lax.axis_index("rep"), lax.axis_index("fsdp")
    x, y, zl, core = rep % 4, shard // 8, (shard // 2) % 4, shard % 2
    z = (rep // 4) * 4 + zl

    def device(x, y, z, core):
        return ((z // 4) * 4 + x, (y * 4 + z % 4) * 2 + core)

    sibling = device(x, y, z, 1 - core)
    x_others = [device((x + d) % 4, y, z, core) for d in (1, 2, 3)]
    y_all = [device(x, (y + d) % 4, z, core) for d in (1, 2, 3)]
    z_all = [device(x, y, (z + d) % 8, core) for d in (1, 2 + 4 * core, 7)]
    z_two_back = device(x, y, (z + 6 + 4 * core) % 8, core)
    z_far = device(x, y, (z + 4) % 8, core)
    at = (x, y, zl, core)
    rings = ((y_all, (y_all[0], y_all[2])), (z_all, (z_all[0], z_all[2])))

    barrier = pltpu.get_barrier_semaphore()
    greeted = [sibling, z_far, z_two_back] + x_others + y_all + z_all
    for other in greeted:
        pl.semaphore_signal(barrier, inc=1, device_id=other, device_id_type=MESH)
    loads = [
        pltpu.make_async_copy(src, dst, local.at[number])
        for number, (src, dst) in enumerate(
            ((wd_in, wd), (wc_in, wc), (ws_in, ws), (img_in, img), (ag_in, ag), (sg_in, sg))
        )
    ]
    for load in loads:
        load.start()
    for load in loads[:3]:
        load.wait()

    def place_shard(buf, values, lane_tile, per_lane, lanes):
        low = lane_tile * 128
        base = per_lane * lane_tile
        if lanes < 128:
            for row in range(ROW_TILES):
                buf[y, zl, core, base + row] = jnp.zeros((16, 128), BF)
            for row in range(ROW_TILES):
                high = min(SHARD, 16 * row + 16)
                buf[y, zl, core, base + row, 0 : high - 16 * row, 0:lanes] = values[16 * row : high, low : low + lanes]
        else:
            full = values[0:80, low : low + 128].reshape(5, 16, 128)
            buf[y, zl, core, base : base + 5] = full
            buf[y, zl, core, base + 5] = jnp.zeros((16, 128), BF)
            buf[y, zl, core, base + 5, 0:10] = values[80:SHARD, low : low + 128]

    for tile in range(3):
        place_shard(ga, wd, tile, 6, min(128, C0 - 128 * tile))
    for tile in range(5):
        place_shard(gb, wc, tile, 7, 128)
        gb[y, zl, core, 7 * tile + 6] = jnp.zeros((16, 128), BF)
        gb[y, zl, core, 7 * tile + 6, 0:SKIP] = ws[:, 128 * tile : 128 * tile + 128]

    pl.semaphore_wait(barrier, len(greeted))

    copies = Copies(sems)
    wa = spreads(copies, "a", ga, TILES_A, at, rings, sibling, slots[0:2])
    wb = spreads(copies, "b", gb, TILES_B, at, rings, sibling, slots[4:6])

    each("s0", *wa)
    each("s0", *wb)

    for number, (tile, tap) in enumerate(PAIRS):
        spread[number] = spread_matrix(tile, tap)
    for load in loads[3:]:
        load.wait()
    padded_img[...] = jnp.zeros((512, LANES0), BF)
    padded_img[:, 0:C0] = img[...]

    each("s1", *wa)
    each("s1", *wb)
    each("s2", *wa)
    each("share", *wa, args=(0,))
    each("s2", *wb)
    each("share", *wb, args=(0,))

    for tap in range(9):
        taps[tap] = dot(shift_down(tap), padded_img[...]).astype(BF)

    def columns(out):
        for tile in range(COLS // TILE):
            total = None
            for number, (tile_of, tap) in enumerate(PAIRS):
                if tile_of == tile:
                    term = dot(taps[tap], spread[number])
                    total = term if total is None else total + term
            out[:, tile * TILE : (tile + 1) * TILE] = total.astype(BF)

    each("s4", *wa)
    each("s5", *wa)
    each("share", *wa, args=(1, 3))
    each("s4", *wb)
    columns(cols_img)
    each("s6", *wa)
    each("share", *wa, args=(2,))
    each("s5", *wb)
    each("share", *wb, args=(1, 3))
    each("end", *wa)

    def chunk_of(q):
        return slice(q * CHUNK, (q + 1) * CHUNK)

    def rows_of(buf, q, lane_tiles, per_lane):
        parts = [
            buf[q, :, :, per_lane * tile : per_lane * tile + ROW_TILES].reshape(CHUNK, 128)
            for tile in range(lane_tiles)
        ]
        return jnp.concatenate(parts, axis=1)

    def down_rows(q):
        return rows_of(ga, q, 3, 6)

    def conv_rows(q):
        return rows_of(gb, q, 5, 7)

    reduced = sum(dot(cols_img[:, chunk_of(q)], down_rows(q)) for q in range(4)).astype(BF)
    same0 = group_matrix(LANES0, group10)
    normed0, scale0 = normalise(reduced.astype(F32), same0, CELLS * (C0 // 32))
    first = silu(normed0).astype(BF)
    for tap in range(9):
        taps[tap] = dot(shift_conv(tap), first).astype(BF)
    columns(cols_first)
    skip_spread = skip_matrix()
    reduced_cols = dot(reduced, skip_spread).astype(BF)
    grad_skip = dot_tn(reduced_cols, sg[...]).astype(BF)
    for tile in range(5):
        grad_b[:, :, :, 7 * tile + 6] = grad_skip[:, 128 * tile : 128 * tile + 128].reshape(4, 4, 2, 16, 128)
    grad_b[:, :, :, 35] = jnp.zeros((4, 4, 2, 16, 128), BF)
    grad_a[:, :, :, 18:20] = jnp.zeros((4, 4, 2, 2, 16, 128), BF)

    each("s6", *wb)
    each("share", *wb, args=(2,))
    each("end", *wb)

    hidden = sum(dot(cols_first[:, chunk_of(q)], conv_rows(q)) for q in range(4)).astype(BF)
    same1 = group_matrix(C1, group20)
    normed1, scale1 = normalise(hidden.astype(F32), same1, CELLS * (C1 // 32))
    act_out[...] = silu(normed1).astype(BF)
    act_store = pltpu.make_async_copy(act_out, act_hbm, local.at[6])
    act_store.start()
    d_hidden = normalise_back(ag[...].astype(F32), normed1, scale1, same1, CELLS * (C1 // 32)).astype(BF)

    devices = (sibling, z_far, x_others)
    back_a = Gradients(copies, "a", grad_a, sib_a, sum_a, slots[:4], TILES_A, at, rings, devices)
    back_b = Gradients(copies, "b", grad_b, sib_b, sum_b, slots[4:], TILES_B, at, rings, devices)

    for q in range(4):
        part = dot_tn(cols_first[:, chunk_of(q)], d_hidden).astype(BF)
        for tile in range(5):
            grad_b[q, :, :, 7 * tile : 7 * tile + 6] = part[:, 128 * tile : 128 * tile + 128].reshape(4, 2, 6, 16, 128)
        back_b.cross(q)

    for q in range(4):
        cols_first[:, chunk_of(q)] = dot_nt(d_hidden, conv_rows(q)).astype(BF)

    back_b.add_cores()
    each("r0", *back_b.routes)

    d_first = jnp.zeros((CELLS, LANES0), F32)
    for tap in range(9):
        part = None
        for number, (tile, tap_of) in enumerate(PAIRS):
            if tap_of == tap:
                term = dot_nt(cols_first[:, tile * TILE : (tile + 1) * TILE], spread[number])
                part = term if part is None else part + term
        d_first = d_first + dot(shift_conv(8 - tap), part.astype(BF))

    skip_rows = jnp.concatenate([gb[:, :, :, 7 * tile + 6].reshape(512, 128) for tile in range(5)], axis=1)
    short_out[...] = dot(reduced_cols, skip_rows).astype(BF)
    short_store = pltpu.make_async_copy(short_out, short_hbm, local.at[7])
    short_store.start()
    d_skip = dot_nt(dot_nt(sg[...], skip_rows).astype(BF), skip_spread)
    d_norm = normalise_back(
        d_first.astype(BF).astype(F32), normed0, scale0, same0, CELLS * (C0 // 32)
    )
    d_reduced = (d_norm + d_skip).astype(BF)

    for q in range(4):
        part = dot_tn(cols_img[:, chunk_of(q)], d_reduced).astype(BF)
        for tile in range(3):
            grad_a[q, :, :, 6 * tile : 6 * tile + 6] = part[:, 128 * tile : 128 * tile + 128].reshape(4, 2, 6, 16, 128)
        back_a.cross(q)

    each("r1", *back_b.routes)
    back_a.add_cores()
    each("r0", *back_a.routes)
    each("r2", *back_b.routes)
    each("r1", *back_a.routes)
    each("r3", *back_b.routes)
    back_b.send_x()
    each("r2", *back_a.routes)
    back_b.send_far()
    each("r3", *back_a.routes)
    back_a.send_x()
    back_b.send_full()
    back_a.send_far()
    back_b.wait_full()
    full_b_out[...] = back_b.full[...]
    back_a.send_full()
    back_a.wait_full()
    full_a_out[...] = back_a.full[...]
    act_store.wait()
    short_store.wait()
    assert len(copies.numbers) == SEMS
    each("drain", *wa, *wb, *back_a.routes, *back_b.routes, back_a, back_b)


def finish(act_in, short_in, full_a, full_b, act_out, short_out, down_out, conv_out, skip_out):
    act_out[...] = act_in[...]
    short_out[...] = short_in[...]

    def rows(full, cut, number, high):
        place = divmod(number, cut.quarter)
        return full[place].astype(F32)[0:high] * (1.0 / 256)

    for tile in range(5):
        lanes = slice(tile * 128, (tile + 1) * 128)
        for row in range(ROW_TILES):
            high = min(SHARD - 16 * row, 16)
            conv_out[16 * row : 16 * row + high, lanes] = rows(full_b, TILES_B, 7 * tile + row, high)
        skip_out[:, lanes] = rows(full_b, TILES_B, 7 * tile + 6, SKIP)
    for tile in range(3):
        wide = min(C0 - tile * 128, 128)
        for row in range(ROW_TILES):
            high = min(SHARD - 16 * row, 16)
            values = rows(full_a, TILES_A, 6 * tile + row, high)
            down_out[16 * row : 16 * row + high, tile * 128 : tile * 128 + wide] = values[:, 0:wide]


def vmem(*shape):
    return pltpu.VMEM(shape, BF)


def tiles(*shape):
    return vmem(*shape, 16, 128)


def body(images, w_down, w_conv, w_skip, act_grad, short_grad):
    picture = images.reshape(512, C0)
    act_cot = act_grad.reshape(CELLS, C1)
    short_cot = short_grad.reshape(CELLS, C1)
    a, b = TILES_A.slots, TILES_B.slots
    slots = []
    for cut in (TILES_A, TILES_B):
        for _, count in cut.routes:
            slots.append(tiles(15, count))
        slots += [tiles(7, cut.quarter), tiles(4, cut.quarter)]

    outs = pl.pallas_call(
        kernel,
        out_shape=(
            jax.ShapeDtypeStruct((CELLS, C1), BF),
            jax.ShapeDtypeStruct((CELLS, C1), BF),
            jax.ShapeDtypeStruct((4, TILES_A.quarter, 16, 128), BF),
            jax.ShapeDtypeStruct((4, TILES_B.quarter, 16, 128), BF),
        ),
        in_specs=[pl.BlockSpec(memory_space=pl.ANY)] * 6,
        out_specs=tuple([pl.BlockSpec(memory_space=pl.ANY)] * 2 + [pl.BlockSpec(memory_space=pltpu.VMEM)] * 2),
        scratch_shapes=[
            vmem(512, C0),
            vmem(SHARD, C0),
            vmem(SHARD, C1),
            vmem(SKIP, C1),
            *[vmem(CELLS, C1)] * 4,
            pltpu.SemaphoreType.DMA((8,)),
            tiles(4, 4, 2, a),
            tiles(4, 4, 2, b),
            tiles(4, 4, 2, a),
            tiles(4, 4, 2, b),
            tiles(4, 4, a),
            tiles(4, 4, b),
            tiles(4, 4, a),
            tiles(4, 4, b),
            vmem(len(PAIRS), LANES0, TILE),
            vmem(512, LANES0),
            vmem(9, CELLS, LANES0),
            vmem(CELLS, COLS),
            vmem(CELLS, COLS),
            pltpu.SemaphoreType.DMA((SEMS,)),
            *slots,
        ],
        compiler_params=pltpu.CompilerParams(
            collective_id=0, has_side_effects=True, vmem_limit_bytes=56 * 1024 * 1024
        ),
    )(picture, w_down, w_conv, w_skip, act_cot, short_cot)
    activated, shortcut, down, conv, skip = pl.pallas_call(
        finish,
        out_shape=(
            jax.ShapeDtypeStruct((CELLS, C1), BF),
            jax.ShapeDtypeStruct((CELLS, C1), BF),
            jax.ShapeDtypeStruct((SHARD, C0), F32),
            jax.ShapeDtypeStruct((SHARD, C1), F32),
            jax.ShapeDtypeStruct((SKIP, C1), F32),
        ),
        in_specs=[pl.BlockSpec(memory_space=pltpu.VMEM)] * 4,
        out_specs=tuple([pl.BlockSpec(memory_space=pltpu.VMEM)] * 5),
    )(*outs)
    return (
        activated.reshape(act_grad.shape),
        shortcut.reshape(short_grad.shape),
        down,
        conv,
        skip,
    )


def solution(mesh):
    cells = P(("rep", "fsdp"), None, None, None)
    rows = P("fsdp", None)
    return jax.shard_map(
        body,
        mesh=mesh,
        in_specs=(cells, rows, rows, rows, cells, cells),
        out_specs=(cells, cells, rows, rows, rows),
        check_vma=False,
    )
```

```python
import jax
import jax.numpy as jnp
from jax import lax
from jax.experimental import pallas as pl
from jax.experimental.pallas import tpu as pltpu
from jax.sharding import PartitionSpec as P

MESH = pl.DeviceIdType.MESH
BF = jnp.bfloat16
F32 = jnp.float32

C0, C1 = 320, 640
LANES0 = 384
SHARD = 90
PAD = 96
SKIP, SKIP_PAD = 10, 16
ROW_TILES = PAD // 16
CELLS = 128
TILE = 256
COLS = 32 * PAD
CHUNK = 8 * PAD
SEMS = 92
EPS = 1e-5


def source_of(col):
    shard, place = divmod(col, PAD)
    return SHARD * shard + place if place < SHARD else -1


def tile_taps():
    pairs = []
    for tile in range(COLS // TILE):
        cols = [source_of(c) for c in range(tile * TILE, (tile + 1) * TILE)]
        for tap in sorted({s // C0 for s in cols if s >= 0}):
            pairs.append((tile, tap))
    return pairs


PAIRS = tile_taps()


def iota(shape, axis):
    return lax.broadcasted_iota(jnp.int32, shape, axis)


def ones_where(mask):
    return jnp.where(mask, 1.0, 0.0).astype(BF)


def spread_matrix(tile, tap):
    lane = iota((1, TILE), 1) + tile * TILE
    shard = jnp.full((1, TILE), tile * TILE // PAD, jnp.int32)
    for edge in range(PAD, COLS, PAD):
        if tile * TILE < edge < (tile + 1) * TILE:
            shard = shard + jnp.where(lane >= edge, 1, 0)
    place = lane - PAD * shard
    channel = lane - (PAD - SHARD) * shard - C0 * tap
    good = (place < SHARD) & (channel >= 0) & (channel < C0)
    channel = jnp.where(good, channel, -1)
    return ones_where(iota((LANES0, TILE), 0) == channel)


def skip_matrix():
    lane = iota((1, 32 * SKIP_PAD), 1)
    shard = lane >> 4
    place = lane - SKIP_PAD * shard
    channel = jnp.where(place < SKIP, SKIP * shard + place, -1)
    return ones_where(iota((LANES0, 32 * SKIP_PAD), 0) == channel)


def shift_down(tap):
    kh, kw = divmod(tap, 3)
    cell = iota((CELLS, 1), 0)
    row, col = 2 * (cell >> 4) + kh - 1, 2 * (cell & 15) + kw - 1
    index = jnp.where((row >= 0) & (col >= 0), row * 32 + col, -1)
    return ones_where(iota((CELLS, 512), 1) == index)


def shift_conv(tap):
    kh, kw = divmod(tap, 3)
    cell = iota((CELLS, 1), 0)
    row, col = (cell >> 4) + kh - 1, (cell & 15) + kw - 1
    good = (row >= 0) & (row < 8) & (col >= 0) & (col < 16)
    index = jnp.where(good, row * 16 + col, -1)
    return ones_where(iota((CELLS, CELLS), 1) == index)


def dot(a, b):
    return lax.dot_general(a, b, (((1,), (0,)), ((), ())), preferred_element_type=F32)


def dot_nt(a, b):
    return lax.dot_general(a, b, (((1,), (1,)), ((), ())), preferred_element_type=F32)


def dot_tn(a, b):
    return lax.dot_general(a, b, (((0,), (0,)), ((), ())), preferred_element_type=F32)


def group_matrix(width, group_of):
    return ones_where(group_of(iota((width, width), 0)) == group_of(iota((width, width), 1)))


def group10(c):
    return (c * 6554) >> 16


def group20(c):
    return (c * 3277) >> 16


def group_sums(vectors, same):
    width = same.shape[0]
    row = iota((8, width), 0)
    stacked = jnp.zeros((8, width), F32)
    for number, vector in enumerate(vectors):
        rest = vector
        for term in range(3):
            part = rest.astype(BF).astype(F32)
            rest = rest - part
            stacked = jnp.where(row == 4 * number + term, part, stacked)
    sums = dot(stacked.astype(BF), same)
    return [jnp.sum(sums[4 * n : 4 * n + 4], axis=0, keepdims=True) for n in range(len(vectors))]


def normalise(values, same, count):
    (total,) = group_sums([jnp.sum(values, axis=0, keepdims=True)], same)
    centred = values - total * (1.0 / count)
    (square,) = group_sums([jnp.sum(centred * centred, axis=0, keepdims=True)], same)
    scale = lax.rsqrt(square * (1.0 / count) + EPS)
    return centred * scale, scale


def normalise_back(cotangent, normed, scale, same, count):
    sig = 1.0 / (1.0 + jnp.exp(-normed))
    slope = cotangent * (sig * (1.0 + normed * (1.0 - sig)))
    first, second = group_sums(
        [jnp.sum(slope, axis=0, keepdims=True), jnp.sum(slope * normed, axis=0, keepdims=True)], same
    )
    return scale * (slope - first * (1.0 / count) - normed * (second * (1.0 / count)))


def silu(normed):
    return normed / (1.0 + jnp.exp(-normed))


class Tiles:
    def __init__(self, count, slots):
        first = (count + 1) // 2
        self.routes = ((0, first), (first, count - first))
        self.slots, self.quarter = slots, slots // 4


TILES_A = Tiles(18, 20)
TILES_B = Tiles(35, 36)


class Copies:
    def __init__(self, sems):
        self.sems, self.numbers = sems, {}

    def sem(self, *key):
        return self.sems.at[self.numbers.setdefault(key, len(self.numbers))]

    def start(self, src, dst, device, send, recv):
        pltpu.make_async_remote_copy(
            src_ref=src,
            dst_ref=dst,
            send_sem=self.sem("send", *send),
            recv_sem=self.sem("recv", *recv),
            device_id=device,
            device_id_type=MESH,
        ).start()

    def wait(self, way, key, ref):
        pltpu.make_async_copy(ref, ref, self.sem(way, *key)).wait()


class Spread:
    def __init__(self, copies, name, piece, row, light, heavy, sibling, other, sent):
        self.copies, self.name, self.piece, self.row, self.sibling = copies, name, piece, row, sibling
        self.light, self.heavy, self.other, self.sent = light, heavy, other, sent

    def send(self, i, j, device, recv):
        ref = self.piece(i, j)
        self.copies.start(ref, ref, device, (self.name,), (self.name, recv))

    def wait(self, recv, ref):
        self.copies.wait("recv", (self.name, recv), ref)

    def both(self, i):
        after, before = {0: ("a0", "rest"), 1: ("rest", "b"), 2: ("a2", "rest"), 3: ("rest", "b")}[i]
        self.send(i, 0, self.heavy[0], after)
        self.send(i, 0, self.heavy[1], before)

    def s0(self):
        for d in (1, 3, 2):
            self.send(0, 0, self.light[d - 1], d)

    def own(self):
        self.both(0)

    def s1(self):
        for d in (1, 3, 2):
            self.wait(d, self.piece(4 - d, 0))
            self.both(4 - d)

    def s2(self):
        self.wait("a0", self.piece(0, 3))
        self.send(0, 3, self.heavy[0], "far")

    def s4(self):
        self.wait("b", self.sent.at[pl.ds(0, 2)])
        for i in (3, 1):
            self.send(i, 1, self.heavy[1], "far2")

    def s5(self):
        self.wait("a2", self.piece(2, 3))
        self.send(2, 3, self.heavy[0], "far3")
        self.wait("rest", self.sent.at[pl.ds(0, 4)])

    def share_far(self, i):
        ref = self.piece(i, 2)
        self.copies.start(ref, ref, self.sibling, (self.name, "core"), (self.name, "core"))

    def s6(self):
        self.wait("far", self.piece(0, 2))
        self.share_far(0)
        self.wait("far2", self.sent.at[pl.ds(0, 2)])
        self.share_far(1)
        self.share_far(3)
        self.wait("far3", self.piece(2, 2))
        self.share_far(2)

    def share(self, *offsets):
        for offset in offsets:
            ref = self.row(offset)
            self.copies.start(ref, ref, self.sibling, (self.name, "core"), (self.name, "core"))

    def end(self):
        self.copies.wait("recv", (self.name, "core"), self.other)

    def drain(self):
        self.copies.wait("send", (self.name, "core"), self.other)
        self.copies.wait("send", (self.name,), self.sent)


def add_into(ref, *others):
    total = ref[...].astype(F32)
    for other in others:
        total = total + other[...].astype(F32)
    ref[...] = total.astype(BF)


class Collect:
    def __init__(self, copies, name, piece, light, heavy, lands):
        self.copies, self.name, self.piece = copies, name, piece
        self.light, self.heavy, self.lands = light, heavy, lands

    def send(self, i, j, land, device, recv):
        self.copies.start(self.piece(i, j), self.lands.at[land], device, (self.name,), (self.name, recv))

    def wait(self, recv, start, count):
        self.copies.wait("recv", (self.name, recv), self.lands.at[pl.ds(start, count)])

    def r0(self):
        after, before = self.heavy
        for slot, (i, device) in enumerate(((2, after), (1, before), (3, before), (0, after))):
            self.send(i, 2, slot, device, ("far", slot // 2))
        for i, j, device in ((2, 3, before), (1, 1, after), (3, 1, after), (0, 3, before)):
            self.send(i, j, 8 + i, device, "near")

    def r1(self):
        after, before = self.heavy
        for slot, (i, j, device) in enumerate(((2, 1, after), (1, 3, before), (3, 3, before), (0, 1, after))):
            if slot % 2 == 0:
                self.wait(("far", slot // 2), slot, 2)
            add_into(self.piece(i, j), self.lands.at[slot])
            self.send(i, j, 4 + slot, device, ("next", slot // 2))

    def r2(self):
        self.wait("near", 8, 4)
        for slot, i in enumerate((2, 1, 3, 0)):
            if slot % 2 == 0:
                self.wait(("next", slot // 2), 4 + slot, 2)
            add_into(self.piece(i, 0), self.lands.at[8 + i], self.lands.at[4 + slot])
            if i > 0:
                self.send(i, 0, 11 + i, self.light[i - 1], "light")

    def r3(self):
        self.wait("light", 12, 3)
        add_into(self.piece(0, 0), *(self.lands.at[slot] for slot in (12, 13, 14)))

    def drain(self):
        self.copies.wait("send", (self.name,), self.lands)


def each(method, *routes, args=()):
    for route in routes:
        getattr(route, method)(*args)


def pieces(buf, cut, at, tail):
    _, y, zl, _ = at
    one, two = (pl.ds(*route) for route in cut.routes)

    def piece0(i, j):
        return buf.at[((y + j) % 4, (zl + i) % 4, *tail, one)]

    def piece1(i, j):
        return buf.at[((y + i) % 4, (zl + j) % 4, *tail, two)]

    def row0(j):
        return buf.at[((y + j) % 4, pl.ds(0, 4), *tail, one)]

    def row1(j):
        return buf.at[(pl.ds(0, 4), (zl + j) % 4, *tail, two)]

    return (piece0, row0), (piece1, row1)


def spreads(copies, name, buf, cut, at, rings, sibling, lands):
    (y_all, y_ring), (z_all, z_ring) = rings
    (piece0, row0), (piece1, row1) = pieces(buf, cut, at, (at[3],))
    other0, other1 = (buf.at[pl.ds(0, 4), pl.ds(0, 4), 1 - at[3], pl.ds(*route)] for route in cut.routes)
    return (
        Spread(copies, (name, 0), piece0, row0, z_all, y_ring, sibling, other0, lands[0]),
        Spread(copies, (name, 1), piece1, row1, y_all, z_ring, sibling, other1, lands[1]),
    )


class Gradients:
    def __init__(self, copies, name, grads, lands, sums, slots, cut, at, rings, devices):
        self.copies, self.grads, self.lands, self.sums, self.cut, self.at = copies, grads, lands, sums, cut, at
        (y_all, y_ring), (z_all, z_ring) = rings
        land0, land1, self.ends, self.full = slots
        self.sibling, self.z_far, self.x_others = devices
        self.name = name
        (piece0, _), (piece1, _) = pieces(sums, cut, at, ())
        self.routes = (
            Collect(copies, (name, 2), piece0, z_all, y_ring, land0),
            Collect(copies, (name, 3), piece1, y_all, z_ring, land1),
        )

    def cross(self, q):
        core, key = self.at[3], (self.name, "cross")
        self.copies.start(self.grads.at[q, :, 1 - core], self.lands.at[q], self.sibling, key, key)

    def add_cores(self):
        core = self.at[3]
        self.copies.wait("recv", (self.name, "cross"), self.lands)
        for q in range(4):
            total = self.grads[q, :, core].astype(F32) + self.lands[q].astype(F32)
            self.sums[q] = total.astype(BF)

    def quarter(self, c):
        _, y, zl, _ = self.at
        return self.sums.at[y, zl, pl.ds(self.cut.quarter * (c % 4), self.cut.quarter)]

    def send_x(self):
        x = self.at[0]
        for d in (1, 2, 3):
            self.copies.start(
                self.quarter(x + d), self.ends.at[d - 1], self.x_others[d - 1], (self.name,), (self.name, "x")
            )

    def send_far(self):
        self.copies.wait("recv", (self.name, "x"), self.ends.at[pl.ds(0, 3)])
        total = self.quarter(self.at[0])[...].astype(F32)
        for slot in range(3):
            total = total + self.ends[slot].astype(F32)
        self.ends[3] = total.astype(BF)
        self.copies.start(self.ends.at[3], self.ends.at[4], self.z_far, (self.name,), (self.name, "z"))

    def send_full(self):
        x = self.at[0]
        self.copies.wait("recv", (self.name, "z"), self.ends.at[4])
        self.full[x] = (self.ends[3].astype(F32) + self.ends[4].astype(F32)).astype(BF)
        mine = self.full.at[x]
        for other in self.x_others:
            self.copies.start(mine, mine, other, (self.name,), (self.name, "full"))

    def wait_full(self):
        self.copies.wait("recv", (self.name, "full"), self.ends.at[pl.ds(0, 3)])

    def drain(self):
        self.copies.wait("send", (self.name, "cross"), self.lands)
        self.copies.wait("send", (self.name,), self.ends)


def kernel(
    img_in, wd_in, wc_in, ws_in, ag_in, sg_in,
    act_hbm, short_hbm, full_a_out, full_b_out,
    img, wd, wc, ws, ag, sg, act_out, short_out, local,
    ga, gb, grad_a, grad_b, sib_a, sib_b, sum_a, sum_b,
    spread, padded_img, taps, cols_img, cols_first,
    sems, *slots,
):
    rep, shard = lax.axis_index("rep"), lax.axis_index("fsdp")
    x, y, zl, core = rep % 4, shard // 8, (shard // 2) % 4, shard % 2
    z = (rep // 4) * 4 + zl

    def device(x, y, z, core):
        return ((z // 4) * 4 + x, (y * 4 + z % 4) * 2 + core)

    sibling = device(x, y, z, 1 - core)
    x_others = [device((x + d) % 4, y, z, core) for d in (1, 2, 3)]
    y_all = [device(x, (y + d) % 4, z, core) for d in (1, 2, 3)]
    z_all = [device(x, y, (z + d) % 8, core) for d in (1, 2 + 4 * core, 7)]
    z_two_back = device(x, y, (z + 6 + 4 * core) % 8, core)
    z_far = device(x, y, (z + 4) % 8, core)
    at = (x, y, zl, core)
    rings = ((y_all, (y_all[0], y_all[2])), (z_all, (z_all[0], z_all[2])))

    barrier = pltpu.get_barrier_semaphore()
    greeted = [sibling, z_far, z_two_back] + x_others + y_all + z_all
    for other in greeted:
        pl.semaphore_signal(barrier, inc=1, device_id=other, device_id_type=MESH)
    loads = [
        pltpu.make_async_copy(src, dst, local.at[number])
        for number, (src, dst) in enumerate(
            ((wd_in, wd), (wc_in, wc), (ws_in, ws), (img_in, img), (ag_in, ag), (sg_in, sg))
        )
    ]
    for load in loads:
        load.start()
    for load in loads[:3]:
        load.wait()

    def place_shard(buf, values, lane_tile, per_lane, lanes):
        low = lane_tile * 128
        base = per_lane * lane_tile
        if lanes < 128:
            for row in range(ROW_TILES):
                buf[y, zl, core, base + row] = jnp.zeros((16, 128), BF)
            for row in range(ROW_TILES):
                high = min(SHARD, 16 * row + 16)
                buf[y, zl, core, base + row, 0 : high - 16 * row, 0:lanes] = values[16 * row : high, low : low + lanes]
        else:
            full = values[0:80, low : low + 128].reshape(5, 16, 128)
            buf[y, zl, core, base : base + 5] = full
            buf[y, zl, core, base + 5] = jnp.zeros((16, 128), BF)
            buf[y, zl, core, base + 5, 0:10] = values[80:SHARD, low : low + 128]

    for tile in range(3):
        place_shard(ga, wd, tile, 6, min(128, C0 - 128 * tile))
    for tile in range(5):
        place_shard(gb, wc, tile, 7, 128)
        gb[y, zl, core, 7 * tile + 6] = jnp.zeros((16, 128), BF)
        gb[y, zl, core, 7 * tile + 6, 0:SKIP] = ws[:, 128 * tile : 128 * tile + 128]

    pl.semaphore_wait(barrier, len(greeted))

    copies = Copies(sems)
    wa = spreads(copies, "a", ga, TILES_A, at, rings, sibling, slots[0:2])
    wb = spreads(copies, "b", gb, TILES_B, at, rings, sibling, slots[4:6])

    each("s0", *wa)
    each("s0", *wb)
    each("own", *wa)
    each("own", *wb)

    for number, (tile, tap) in enumerate(PAIRS):
        spread[number] = spread_matrix(tile, tap)
    for load in loads[3:]:
        load.wait()
    padded_img[...] = jnp.zeros((512, LANES0), BF)
    padded_img[:, 0:C0] = img[...]

    each("s1", *wa)
    each("s1", *wb)
    each("s2", *wa)
    each("share", *wa, args=(0,))
    each("s2", *wb)
    each("share", *wb, args=(0,))

    for tap in range(9):
        taps[tap] = dot(shift_down(tap), padded_img[...]).astype(BF)

    def columns(out):
        for tile in range(COLS // TILE):
            total = None
            for number, (tile_of, tap) in enumerate(PAIRS):
                if tile_of == tile:
                    term = dot(taps[tap], spread[number])
                    total = term if total is None else total + term
            out[:, tile * TILE : (tile + 1) * TILE] = total.astype(BF)

    each("s4", *wa)
    each("s5", *wa)
    each("share", *wa, args=(1, 3))
    each("s4", *wb)
    columns(cols_img)
    each("s6", *wa)
    each("s5", *wb)
    each("share", *wb, args=(1, 3))
    each("end", *wa)

    def chunk_of(q):
        return slice(q * CHUNK, (q + 1) * CHUNK)

    def rows_of(buf, q, lane_tiles, per_lane):
        parts = [
            buf[q, :, :, per_lane * tile : per_lane * tile + ROW_TILES].reshape(CHUNK, 128)
            for tile in range(lane_tiles)
        ]
        return jnp.concatenate(parts, axis=1)

    def down_rows(q):
        return rows_of(ga, q, 3, 6)

    def conv_rows(q):
        return rows_of(gb, q, 5, 7)

    reduced = sum(dot(cols_img[:, chunk_of(q)], down_rows(q)) for q in range(4)).astype(BF)
    same0 = group_matrix(LANES0, group10)
    normed0, scale0 = normalise(reduced.astype(F32), same0, CELLS * (C0 // 32))
    first = silu(normed0).astype(BF)
    for tap in range(9):
        taps[tap] = dot(shift_conv(tap), first).astype(BF)
    columns(cols_first)
    skip_spread = skip_matrix()
    reduced_cols = dot(reduced, skip_spread).astype(BF)
    grad_skip = dot_tn(reduced_cols, sg[...]).astype(BF)
    for tile in range(5):
        grad_b[:, :, :, 7 * tile + 6] = grad_skip[:, 128 * tile : 128 * tile + 128].reshape(4, 4, 2, 16, 128)
    grad_b[:, :, :, 35] = jnp.zeros((4, 4, 2, 16, 128), BF)
    grad_a[:, :, :, 18:20] = jnp.zeros((4, 4, 2, 2, 16, 128), BF)

    each("s6", *wb)
    each("end", *wb)

    hidden = sum(dot(cols_first[:, chunk_of(q)], conv_rows(q)) for q in range(4)).astype(BF)
    same1 = group_matrix(C1, group20)
    normed1, scale1 = normalise(hidden.astype(F32), same1, CELLS * (C1 // 32))
    act_out[...] = silu(normed1).astype(BF)
    act_store = pltpu.make_async_copy(act_out, act_hbm, local.at[6])
    act_store.start()
    d_hidden = normalise_back(ag[...].astype(F32), normed1, scale1, same1, CELLS * (C1 // 32)).astype(BF)

    devices = (sibling, z_far, x_others)
    back_a = Gradients(copies, "a", grad_a, sib_a, sum_a, slots[:4], TILES_A, at, rings, devices)
    back_b = Gradients(copies, "b", grad_b, sib_b, sum_b, slots[4:], TILES_B, at, rings, devices)

    for q in range(4):
        part = dot_tn(cols_first[:, chunk_of(q)], d_hidden).astype(BF)
        for tile in range(5):
            grad_b[q, :, :, 7 * tile : 7 * tile + 6] = part[:, 128 * tile : 128 * tile + 128].reshape(4, 2, 6, 16, 128)
        back_b.cross(q)

    for q in range(4):
        cols_first[:, chunk_of(q)] = dot_nt(d_hidden, conv_rows(q)).astype(BF)

    d_first = jnp.zeros((CELLS, LANES0), F32)
    for tap in range(9):
        part = None
        for number, (tile, tap_of) in enumerate(PAIRS):
            if tap_of == tap:
                term = dot_nt(cols_first[:, tile * TILE : (tile + 1) * TILE], spread[number])
                part = term if part is None else part + term
        d_first = d_first + dot(shift_conv(8 - tap), part.astype(BF))

    skip_rows = jnp.concatenate([gb[:, :, :, 7 * tile + 6].reshape(512, 128) for tile in range(5)], axis=1)
    short_out[...] = dot(reduced_cols, skip_rows).astype(BF)
    short_store = pltpu.make_async_copy(short_out, short_hbm, local.at[7])
    short_store.start()
    d_skip = dot_nt(dot_nt(sg[...], skip_rows).astype(BF), skip_spread)
    back_b.add_cores()
    each("r0", *back_b.routes)

    d_norm = normalise_back(
        d_first.astype(BF).astype(F32), normed0, scale0, same0, CELLS * (C0 // 32)
    )
    d_reduced = (d_norm + d_skip).astype(BF)

    for q in range(4):
        part = dot_tn(cols_img[:, chunk_of(q)], d_reduced).astype(BF)
        for tile in range(3):
            grad_a[q, :, :, 6 * tile : 6 * tile + 6] = part[:, 128 * tile : 128 * tile + 128].reshape(4, 2, 6, 16, 128)
        back_a.cross(q)

    each("r1", *back_b.routes)
    back_a.add_cores()
    each("r0", *back_a.routes)
    each("r2", *back_b.routes)
    each("r1", *back_a.routes)
    each("r3", *back_b.routes)
    back_b.send_x()
    each("r2", *back_a.routes)
    back_b.send_far()
    each("r3", *back_a.routes)
    back_a.send_x()
    back_a.send_far()
    back_b.send_full()
    back_b.wait_full()
    full_b_out[...] = back_b.full[...]
    back_a.send_full()
    back_a.wait_full()
    full_a_out[...] = back_a.full[...]
    act_store.wait()
    short_store.wait()
    assert len(copies.numbers) == SEMS
    each("drain", *wa, *wb, *back_a.routes, *back_b.routes, back_a, back_b)


def finish(act_in, short_in, full_a, full_b, act_out, short_out, down_out, conv_out, skip_out):
    act_out[...] = act_in[...]
    short_out[...] = short_in[...]

    def rows(full, cut, number, high):
        place = divmod(number, cut.quarter)
        return full[place].astype(F32)[0:high] * (1.0 / 256)

    for tile in range(5):
        lanes = slice(tile * 128, (tile + 1) * 128)
        for row in range(ROW_TILES):
            high = min(SHARD - 16 * row, 16)
            conv_out[16 * row : 16 * row + high, lanes] = rows(full_b, TILES_B, 7 * tile + row, high)
        skip_out[:, lanes] = rows(full_b, TILES_B, 7 * tile + 6, SKIP)
    for tile in range(3):
        wide = min(C0 - tile * 128, 128)
        for row in range(ROW_TILES):
            high = min(SHARD - 16 * row, 16)
            values = rows(full_a, TILES_A, 6 * tile + row, high)
            down_out[16 * row : 16 * row + high, tile * 128 : tile * 128 + wide] = values[:, 0:wide]


def vmem(*shape):
    return pltpu.VMEM(shape, BF)


def tiles(*shape):
    return vmem(*shape, 16, 128)


def body(images, w_down, w_conv, w_skip, act_grad, short_grad):
    picture = images.reshape(512, C0)
    act_cot = act_grad.reshape(CELLS, C1)
    short_cot = short_grad.reshape(CELLS, C1)
    a, b = TILES_A.slots, TILES_B.slots
    slots = []
    for cut in (TILES_A, TILES_B):
        for _, count in cut.routes:
            slots.append(tiles(15, count))
        slots += [tiles(7, cut.quarter), tiles(4, cut.quarter)]

    outs = pl.pallas_call(
        kernel,
        out_shape=(
            jax.ShapeDtypeStruct((CELLS, C1), BF),
            jax.ShapeDtypeStruct((CELLS, C1), BF),
            jax.ShapeDtypeStruct((4, TILES_A.quarter, 16, 128), BF),
            jax.ShapeDtypeStruct((4, TILES_B.quarter, 16, 128), BF),
        ),
        in_specs=[pl.BlockSpec(memory_space=pl.ANY)] * 6,
        out_specs=tuple([pl.BlockSpec(memory_space=pl.ANY)] * 2 + [pl.BlockSpec(memory_space=pltpu.VMEM)] * 2),
        scratch_shapes=[
            vmem(512, C0),
            vmem(SHARD, C0),
            vmem(SHARD, C1),
            vmem(SKIP, C1),
            *[vmem(CELLS, C1)] * 4,
            pltpu.SemaphoreType.DMA((8,)),
            tiles(4, 4, 2, a),
            tiles(4, 4, 2, b),
            tiles(4, 4, 2, a),
            tiles(4, 4, 2, b),
            tiles(4, 4, a),
            tiles(4, 4, b),
            tiles(4, 4, a),
            tiles(4, 4, b),
            vmem(len(PAIRS), LANES0, TILE),
            vmem(512, LANES0),
            vmem(9, CELLS, LANES0),
            vmem(CELLS, COLS),
            vmem(CELLS, COLS),
            pltpu.SemaphoreType.DMA((SEMS,)),
            *slots,
        ],
        compiler_params=pltpu.CompilerParams(
            collective_id=0, has_side_effects=True, vmem_limit_bytes=56 * 1024 * 1024
        ),
    )(picture, w_down, w_conv, w_skip, act_cot, short_cot)
    activated, shortcut, down, conv, skip = pl.pallas_call(
        finish,
        out_shape=(
            jax.ShapeDtypeStruct((CELLS, C1), BF),
            jax.ShapeDtypeStruct((CELLS, C1), BF),
            jax.ShapeDtypeStruct((SHARD, C0), F32),
            jax.ShapeDtypeStruct((SHARD, C1), F32),
            jax.ShapeDtypeStruct((SKIP, C1), F32),
        ),
        in_specs=[pl.BlockSpec(memory_space=pltpu.VMEM)] * 4,
        out_specs=tuple([pl.BlockSpec(memory_space=pltpu.VMEM)] * 5),
    )(*outs)
    return (
        activated.reshape(act_grad.shape),
        shortcut.reshape(short_grad.shape),
        down,
        conv,
        skip,
    )


def solution(mesh):
    cells = P(("rep", "fsdp"), None, None, None)
    rows = P("fsdp", None)
    return jax.shard_map(
        body,
        mesh=mesh,
        in_specs=(cells, rows, rows, rows, cells, cells),
        out_specs=(cells, cells, rows, rows, rows),
        check_vma=False,
    )
```

```python
import jax
import jax.numpy as jnp
from jax import lax
from jax.experimental import pallas as pl
from jax.experimental.pallas import tpu as pltpu
from jax.sharding import PartitionSpec as P

MESH = pl.DeviceIdType.MESH
BF = jnp.bfloat16
F32 = jnp.float32

C0, C1 = 320, 640
LANES0 = 384
SHARD = 90
PAD = 96
SKIP, SKIP_PAD = 10, 16
ROW_TILES = PAD // 16
CELLS = 128
TILE = 256
COLS = 32 * PAD
CHUNK = 8 * PAD
SEMS = 92
EPS = 1e-5


def source_of(col):
    shard, place = divmod(col, PAD)
    return SHARD * shard + place if place < SHARD else -1


def tile_taps():
    pairs = []
    for tile in range(COLS // TILE):
        cols = [source_of(c) for c in range(tile * TILE, (tile + 1) * TILE)]
        for tap in sorted({s // C0 for s in cols if s >= 0}):
            pairs.append((tile, tap))
    return pairs


PAIRS = tile_taps()


def iota(shape, axis):
    return lax.broadcasted_iota(jnp.int32, shape, axis)


def ones_where(mask):
    return jnp.where(mask, 1.0, 0.0).astype(BF)


def spread_matrix(tile, tap):
    lane = iota((1, TILE), 1) + tile * TILE
    shard = jnp.full((1, TILE), tile * TILE // PAD, jnp.int32)
    for edge in range(PAD, COLS, PAD):
        if tile * TILE < edge < (tile + 1) * TILE:
            shard = shard + jnp.where(lane >= edge, 1, 0)
    place = lane - PAD * shard
    channel = lane - (PAD - SHARD) * shard - C0 * tap
    good = (place < SHARD) & (channel >= 0) & (channel < C0)
    channel = jnp.where(good, channel, -1)
    return ones_where(iota((LANES0, TILE), 0) == channel)


def skip_matrix():
    lane = iota((1, 32 * SKIP_PAD), 1)
    shard = lane >> 4
    place = lane - SKIP_PAD * shard
    channel = jnp.where(place < SKIP, SKIP * shard + place, -1)
    return ones_where(iota((LANES0, 32 * SKIP_PAD), 0) == channel)


def shift_down(tap):
    kh, kw = divmod(tap, 3)
    cell = iota((CELLS, 1), 0)
    row, col = 2 * (cell >> 4) + kh - 1, 2 * (cell & 15) + kw - 1
    index = jnp.where((row >= 0) & (col >= 0), row * 32 + col, -1)
    return ones_where(iota((CELLS, 512), 1) == index)


def shift_conv(tap):
    kh, kw = divmod(tap, 3)
    cell = iota((CELLS, 1), 0)
    row, col = (cell >> 4) + kh - 1, (cell & 15) + kw - 1
    good = (row >= 0) & (row < 8) & (col >= 0) & (col < 16)
    index = jnp.where(good, row * 16 + col, -1)
    return ones_where(iota((CELLS, CELLS), 1) == index)


def dot(a, b):
    return lax.dot_general(a, b, (((1,), (0,)), ((), ())), preferred_element_type=F32)


def dot_nt(a, b):
    return lax.dot_general(a, b, (((1,), (1,)), ((), ())), preferred_element_type=F32)


def dot_tn(a, b):
    return lax.dot_general(a, b, (((0,), (0,)), ((), ())), preferred_element_type=F32)


def group_matrix(width, group_of):
    return ones_where(group_of(iota((width, width), 0)) == group_of(iota((width, width), 1)))


def group10(c):
    return (c * 6554) >> 16


def group20(c):
    return (c * 3277) >> 16


def group_sums(vectors, same):
    width = same.shape[0]
    row = iota((8, width), 0)
    stacked = jnp.zeros((8, width), F32)
    for number, vector in enumerate(vectors):
        rest = vector
        for term in range(3):
            part = rest.astype(BF).astype(F32)
            rest = rest - part
            stacked = jnp.where(row == 4 * number + term, part, stacked)
    sums = dot(stacked.astype(BF), same)
    return [jnp.sum(sums[4 * n : 4 * n + 4], axis=0, keepdims=True) for n in range(len(vectors))]


def normalise(values, same, count):
    (total,) = group_sums([jnp.sum(values, axis=0, keepdims=True)], same)
    centred = values - total * (1.0 / count)
    (square,) = group_sums([jnp.sum(centred * centred, axis=0, keepdims=True)], same)
    scale = lax.rsqrt(square * (1.0 / count) + EPS)
    return centred * scale, scale


def normalise_back(cotangent, normed, scale, same, count):
    sig = 1.0 / (1.0 + jnp.exp(-normed))
    slope = cotangent * (sig * (1.0 + normed * (1.0 - sig)))
    first, second = group_sums(
        [jnp.sum(slope, axis=0, keepdims=True), jnp.sum(slope * normed, axis=0, keepdims=True)], same
    )
    return scale * (slope - first * (1.0 / count) - normed * (second * (1.0 / count)))


def silu(normed):
    return normed / (1.0 + jnp.exp(-normed))


class Tiles:
    def __init__(self, count, slots):
        first = (count + 1) // 2
        self.routes = ((0, first), (first, count - first))
        self.slots, self.quarter = slots, slots // 4


TILES_A = Tiles(18, 20)
TILES_B = Tiles(35, 36)


class Copies:
    def __init__(self, sems):
        self.sems, self.numbers = sems, {}

    def sem(self, *key):
        return self.sems.at[self.numbers.setdefault(key, len(self.numbers))]

    def start(self, src, dst, device, send, recv):
        pltpu.make_async_remote_copy(
            src_ref=src,
            dst_ref=dst,
            send_sem=self.sem("send", *send),
            recv_sem=self.sem("recv", *recv),
            device_id=device,
            device_id_type=MESH,
        ).start()

    def wait(self, way, key, ref):
        pltpu.make_async_copy(ref, ref, self.sem(way, *key)).wait()


class Spread:
    def __init__(self, copies, name, piece, row, light, heavy, sibling, other, sent):
        self.copies, self.name, self.piece, self.row, self.sibling = copies, name, piece, row, sibling
        self.light, self.heavy, self.other, self.sent = light, heavy, other, sent

    def send(self, i, j, device, recv):
        ref = self.piece(i, j)
        self.copies.start(ref, ref, device, (self.name,), (self.name, recv))

    def wait(self, recv, ref):
        self.copies.wait("recv", (self.name, recv), ref)

    def both(self, i):
        after, before = {0: ("a0", "rest"), 1: ("rest", "b"), 2: ("a2", "rest"), 3: ("rest", "b")}[i]
        self.send(i, 0, self.heavy[0], after)
        self.send(i, 0, self.heavy[1], before)

    def s0(self):
        for d in (1, 3, 2):
            self.send(0, 0, self.light[d - 1], d)

    def own(self):
        self.both(0)

    def s1(self):
        for d in (1, 3, 2):
            self.wait(d, self.piece(4 - d, 0))
            self.both(4 - d)

    def s2(self):
        self.wait("a0", self.piece(0, 3))
        self.send(0, 3, self.heavy[0], "far")

    def s4(self):
        self.wait("b", self.sent.at[pl.ds(0, 2)])
        for i in (3, 1):
            self.send(i, 1, self.heavy[1], "far2")

    def s5(self):
        self.wait("a2", self.piece(2, 3))
        self.send(2, 3, self.heavy[0], "far3")
        self.wait("rest", self.sent.at[pl.ds(0, 4)])

    def share_far(self, i):
        ref = self.piece(i, 2)
        self.copies.start(ref, ref, self.sibling, (self.name, "core"), (self.name, "core"))

    def s6(self):
        self.wait("far", self.piece(0, 2))
        self.share_far(0)
        self.wait("far2", self.sent.at[pl.ds(0, 2)])
        self.share_far(1)
        self.share_far(3)
        self.wait("far3", self.piece(2, 2))
        self.share_far(2)

    def share(self, *offsets):
        for offset in offsets:
            ref = self.row(offset)
            self.copies.start(ref, ref, self.sibling, (self.name, "core"), (self.name, "core"))

    def end(self):
        self.copies.wait("recv", (self.name, "core"), self.other)

    def drain(self):
        self.copies.wait("send", (self.name, "core"), self.other)
        self.copies.wait("send", (self.name,), self.sent)


def add_into(ref, *others):
    total = ref[...].astype(F32)
    for other in others:
        total = total + other[...].astype(F32)
    ref[...] = total.astype(BF)


class Collect:
    def __init__(self, copies, name, piece, light, heavy, lands):
        self.copies, self.name, self.piece = copies, name, piece
        self.light, self.heavy, self.lands = light, heavy, lands

    def send(self, i, j, land, device, recv):
        self.copies.start(self.piece(i, j), self.lands.at[land], device, (self.name,), (self.name, recv))

    def wait(self, recv, start, count):
        self.copies.wait("recv", (self.name, recv), self.lands.at[pl.ds(start, count)])

    def r0(self):
        after, before = self.heavy
        for slot, (i, device) in enumerate(((2, after), (1, before), (3, before), (0, after))):
            self.send(i, 2, slot, device, ("far", slot // 2))
        for i, j, device in ((2, 3, before), (1, 1, after), (3, 1, after), (0, 3, before)):
            self.send(i, j, 8 + i, device, "near")

    def r1(self):
        after, before = self.heavy
        for slot, (i, j, device) in enumerate(((2, 1, after), (1, 3, before), (3, 3, before), (0, 1, after))):
            if slot % 2 == 0:
                self.wait(("far", slot // 2), slot, 2)
            add_into(self.piece(i, j), self.lands.at[slot])
            self.send(i, j, 4 + slot, device, ("next", slot // 2))

    def r2(self):
        self.wait("near", 8, 4)
        for slot, i in enumerate((2, 1, 3, 0)):
            if slot % 2 == 0:
                self.wait(("next", slot // 2), 4 + slot, 2)
            add_into(self.piece(i, 0), self.lands.at[8 + i], self.lands.at[4 + slot])
            if i > 0:
                self.send(i, 0, 11 + i, self.light[i - 1], "light")

    def r3(self):
        self.wait("light", 12, 3)
        add_into(self.piece(0, 0), *(self.lands.at[slot] for slot in (12, 13, 14)))

    def drain(self):
        self.copies.wait("send", (self.name,), self.lands)


def each(method, *routes, args=()):
    for route in routes:
        getattr(route, method)(*args)


def pieces(buf, cut, at, tail):
    _, y, zl, _ = at
    one, two = (pl.ds(*route) for route in cut.routes)

    def piece0(i, j):
        return buf.at[((y + j) % 4, (zl + i) % 4, *tail, one)]

    def piece1(i, j):
        return buf.at[((y + i) % 4, (zl + j) % 4, *tail, two)]

    def row0(j):
        return buf.at[((y + j) % 4, pl.ds(0, 4), *tail, one)]

    def row1(j):
        return buf.at[(pl.ds(0, 4), (zl + j) % 4, *tail, two)]

    return (piece0, row0), (piece1, row1)


def spreads(copies, name, buf, cut, at, rings, sibling, lands):
    (y_all, y_ring), (z_all, z_ring) = rings
    (piece0, row0), (piece1, row1) = pieces(buf, cut, at, (at[3],))
    other0, other1 = (buf.at[pl.ds(0, 4), pl.ds(0, 4), 1 - at[3], pl.ds(*route)] for route in cut.routes)
    return (
        Spread(copies, (name, 0), piece0, row0, z_all, y_ring, sibling, other0, lands[0]),
        Spread(copies, (name, 1), piece1, row1, y_all, z_ring, sibling, other1, lands[1]),
    )


class Gradients:
    def __init__(self, copies, name, grads, lands, sums, slots, cut, at, rings, devices):
        self.copies, self.grads, self.lands, self.sums, self.cut, self.at = copies, grads, lands, sums, cut, at
        (y_all, y_ring), (z_all, z_ring) = rings
        land0, land1, self.ends, self.full = slots
        self.sibling, self.z_far, self.x_others = devices
        self.name = name
        (piece0, _), (piece1, _) = pieces(sums, cut, at, ())
        self.routes = (
            Collect(copies, (name, 2), piece0, z_all, y_ring, land0),
            Collect(copies, (name, 3), piece1, y_all, z_ring, land1),
        )

    def cross(self, q):
        core, key = self.at[3], (self.name, "cross")
        self.copies.start(self.grads.at[q, :, 1 - core], self.lands.at[q], self.sibling, key, key)

    def add_cores(self):
        core = self.at[3]
        self.copies.wait("recv", (self.name, "cross"), self.lands)
        for q in range(4):
            total = self.grads[q, :, core].astype(F32) + self.lands[q].astype(F32)
            self.sums[q] = total.astype(BF)

    def quarter(self, c):
        _, y, zl, _ = self.at
        return self.sums.at[y, zl, pl.ds(self.cut.quarter * (c % 4), self.cut.quarter)]

    def send_x(self):
        x = self.at[0]
        for d in (1, 2, 3):
            self.copies.start(
                self.quarter(x + d), self.ends.at[d - 1], self.x_others[d - 1], (self.name,), (self.name, "x")
            )

    def send_far(self):
        self.copies.wait("recv", (self.name, "x"), self.ends.at[pl.ds(0, 3)])
        total = self.quarter(self.at[0])[...].astype(F32)
        for slot in range(3):
            total = total + self.ends[slot].astype(F32)
        self.ends[3] = total.astype(BF)
        self.copies.start(self.ends.at[3], self.ends.at[4], self.z_far, (self.name,), (self.name, "z"))

    def send_full(self):
        x = self.at[0]
        self.copies.wait("recv", (self.name, "z"), self.ends.at[4])
        self.full[x] = (self.ends[3].astype(F32) + self.ends[4].astype(F32)).astype(BF)
        mine = self.full.at[x]
        for other in self.x_others:
            self.copies.start(mine, mine, other, (self.name,), (self.name, "full"))

    def wait_full(self):
        self.copies.wait("recv", (self.name, "full"), self.ends.at[pl.ds(0, 3)])

    def drain(self):
        self.copies.wait("send", (self.name, "cross"), self.lands)
        self.copies.wait("send", (self.name,), self.ends)


def kernel(
    img_in, wd_in, wc_in, ws_in, ag_in, sg_in,
    act_hbm, short_hbm, full_a_out, full_b_out,
    img, wd, wc, ws, ag, sg, act_out, short_out, local,
    ga, gb, grad_a, grad_b, sib_a, sib_b, sum_a, sum_b,
    spread, padded_img, taps, cols_img, cols_first, same0, same1, skip_spread,
    sems, *slots,
):
    rep, shard = lax.axis_index("rep"), lax.axis_index("fsdp")
    x, y, zl, core = rep % 4, shard // 8, (shard // 2) % 4, shard % 2
    z = (rep // 4) * 4 + zl

    def device(x, y, z, core):
        return ((z // 4) * 4 + x, (y * 4 + z % 4) * 2 + core)

    sibling = device(x, y, z, 1 - core)
    x_others = [device((x + d) % 4, y, z, core) for d in (1, 2, 3)]
    y_all = [device(x, (y + d) % 4, z, core) for d in (1, 2, 3)]
    z_all = [device(x, y, (z + d) % 8, core) for d in (1, 2 + 4 * core, 7)]
    z_two_back = device(x, y, (z + 6 + 4 * core) % 8, core)
    z_far = device(x, y, (z + 4) % 8, core)
    at = (x, y, zl, core)
    rings = ((y_all, (y_all[0], y_all[2])), (z_all, (z_all[0], z_all[2])))

    barrier = pltpu.get_barrier_semaphore()
    greeted = [sibling, z_far, z_two_back] + x_others + y_all + z_all
    for other in greeted:
        pl.semaphore_signal(barrier, inc=1, device_id=other, device_id_type=MESH)
    loads = [
        pltpu.make_async_copy(src, dst, local.at[number])
        for number, (src, dst) in enumerate(
            ((wd_in, wd), (wc_in, wc), (ws_in, ws), (img_in, img), (ag_in, ag), (sg_in, sg))
        )
    ]
    for load in loads:
        load.start()
    for load in loads[:3]:
        load.wait()

    def place_shard(buf, values, lane_tile, per_lane, lanes):
        low = lane_tile * 128
        base = per_lane * lane_tile
        if lanes < 128:
            for row in range(ROW_TILES):
                buf[y, zl, core, base + row] = jnp.zeros((16, 128), BF)
            for row in range(ROW_TILES):
                high = min(SHARD, 16 * row + 16)
                buf[y, zl, core, base + row, 0 : high - 16 * row, 0:lanes] = values[16 * row : high, low : low + lanes]
        else:
            full = values[0:80, low : low + 128].reshape(5, 16, 128)
            buf[y, zl, core, base : base + 5] = full
            buf[y, zl, core, base + 5] = jnp.zeros((16, 128), BF)
            buf[y, zl, core, base + 5, 0:10] = values[80:SHARD, low : low + 128]

    for tile in range(3):
        place_shard(ga, wd, tile, 6, min(128, C0 - 128 * tile))
    for tile in range(5):
        place_shard(gb, wc, tile, 7, 128)
        gb[y, zl, core, 7 * tile + 6] = jnp.zeros((16, 128), BF)
        gb[y, zl, core, 7 * tile + 6, 0:SKIP] = ws[:, 128 * tile : 128 * tile + 128]

    pl.semaphore_wait(barrier, len(greeted))

    copies = Copies(sems)
    wa = spreads(copies, "a", ga, TILES_A, at, rings, sibling, slots[0:2])
    wb = spreads(copies, "b", gb, TILES_B, at, rings, sibling, slots[4:6])

    each("s0", *wa)
    each("s0", *wb)
    each("own", *wa)
    each("own", *wb)

    for number, (tile, tap) in enumerate(PAIRS):
        spread[number] = spread_matrix(tile, tap)
    same0[...] = group_matrix(LANES0, group10)
    same1[...] = group_matrix(C1, group20)
    skip_spread[...] = skip_matrix()
    for load in loads[3:]:
        load.wait()
    padded_img[...] = jnp.zeros((512, LANES0), BF)
    padded_img[:, 0:C0] = img[...]

    each("s1", *wa)
    each("s1", *wb)
    each("s2", *wa)
    each("share", *wa, args=(0,))
    each("s2", *wb)
    each("share", *wb, args=(0,))

    for tap in range(9):
        taps[tap] = dot(shift_down(tap), padded_img[...]).astype(BF)

    def columns(out):
        for tile in range(COLS // TILE):
            total = None
            for number, (tile_of, tap) in enumerate(PAIRS):
                if tile_of == tile:
                    term = dot(taps[tap], spread[number])
                    total = term if total is None else total + term
            out[:, tile * TILE : (tile + 1) * TILE] = total.astype(BF)

    each("s4", *wa)
    each("s5", *wa)
    each("share", *wa, args=(1, 3))
    each("s4", *wb)
    columns(cols_img)
    each("s6", *wa)
    each("s5", *wb)
    each("share", *wb, args=(1, 3))
    each("end", *wa)

    def chunk_of(q):
        return slice(q * CHUNK, (q + 1) * CHUNK)

    def rows_of(buf, q, lane_tiles, per_lane):
        parts = [
            buf[q, :, :, per_lane * tile : per_lane * tile + ROW_TILES].reshape(CHUNK, 128)
            for tile in range(lane_tiles)
        ]
        return jnp.concatenate(parts, axis=1)

    def down_rows(q):
        return rows_of(ga, q, 3, 6)

    def conv_rows(q):
        return rows_of(gb, q, 5, 7)

    reduced = sum(dot(cols_img[:, chunk_of(q)], down_rows(q)) for q in range(4)).astype(BF)
    normed0, scale0 = normalise(reduced.astype(F32), same0[...], CELLS * (C0 // 32))
    first = silu(normed0).astype(BF)
    for tap in range(9):
        taps[tap] = dot(shift_conv(tap), first).astype(BF)
    columns(cols_first)
    reduced_cols = dot(reduced, skip_spread[...]).astype(BF)
    grad_skip = dot_tn(reduced_cols, sg[...]).astype(BF)
    for tile in range(5):
        grad_b[:, :, :, 7 * tile + 6] = grad_skip[:, 128 * tile : 128 * tile + 128].reshape(4, 4, 2, 16, 128)
    grad_b[:, :, :, 35] = jnp.zeros((4, 4, 2, 16, 128), BF)
    grad_a[:, :, :, 18:20] = jnp.zeros((4, 4, 2, 2, 16, 128), BF)

    each("s6", *wb)
    each("end", *wb)

    hidden = sum(dot(cols_first[:, chunk_of(q)], conv_rows(q)) for q in range(4)).astype(BF)
    normed1, scale1 = normalise(hidden.astype(F32), same1[...], CELLS * (C1 // 32))
    act_out[...] = silu(normed1).astype(BF)
    act_store = pltpu.make_async_copy(act_out, act_hbm, local.at[6])
    act_store.start()
    d_hidden = normalise_back(ag[...].astype(F32), normed1, scale1, same1[...], CELLS * (C1 // 32)).astype(BF)

    devices = (sibling, z_far, x_others)
    back_a = Gradients(copies, "a", grad_a, sib_a, sum_a, slots[:4], TILES_A, at, rings, devices)
    back_b = Gradients(copies, "b", grad_b, sib_b, sum_b, slots[4:], TILES_B, at, rings, devices)

    for q in range(4):
        part = dot_tn(cols_first[:, chunk_of(q)], d_hidden).astype(BF)
        for tile in range(5):
            grad_b[q, :, :, 7 * tile : 7 * tile + 6] = part[:, 128 * tile : 128 * tile + 128].reshape(4, 2, 6, 16, 128)
        back_b.cross(q)

    for q in range(4):
        cols_first[:, chunk_of(q)] = dot_nt(d_hidden, conv_rows(q)).astype(BF)

    d_first = jnp.zeros((CELLS, LANES0), F32)
    for tap in range(9):
        part = None
        for number, (tile, tap_of) in enumerate(PAIRS):
            if tap_of == tap:
                term = dot_nt(cols_first[:, tile * TILE : (tile + 1) * TILE], spread[number])
                part = term if part is None else part + term
        d_first = d_first + dot(shift_conv(8 - tap), part.astype(BF))

    skip_rows = jnp.concatenate([gb[:, :, :, 7 * tile + 6].reshape(512, 128) for tile in range(5)], axis=1)
    short_out[...] = dot(reduced_cols, skip_rows).astype(BF)
    short_store = pltpu.make_async_copy(short_out, short_hbm, local.at[7])
    short_store.start()
    d_skip = dot_nt(dot_nt(sg[...], skip_rows).astype(BF), skip_spread[...])
    back_b.add_cores()
    each("r0", *back_b.routes)

    d_norm = normalise_back(
        d_first.astype(BF).astype(F32), normed0, scale0, same0[...], CELLS * (C0 // 32)
    )
    d_reduced = (d_norm + d_skip).astype(BF)

    for q in range(4):
        part = dot_tn(cols_img[:, chunk_of(q)], d_reduced).astype(BF)
        for tile in range(3):
            grad_a[q, :, :, 6 * tile : 6 * tile + 6] = part[:, 128 * tile : 128 * tile + 128].reshape(4, 2, 6, 16, 128)
        back_a.cross(q)

    each("r1", *back_b.routes)
    back_a.add_cores()
    each("r0", *back_a.routes)
    each("r2", *back_b.routes)
    each("r1", *back_a.routes)
    each("r3", *back_b.routes)
    back_b.send_x()
    each("r2", *back_a.routes)
    back_b.send_far()
    each("r3", *back_a.routes)
    back_a.send_x()
    back_a.send_far()
    back_b.send_full()
    back_b.wait_full()
    full_b_out[...] = back_b.full[...]
    back_a.send_full()
    back_a.wait_full()
    full_a_out[...] = back_a.full[...]
    act_store.wait()
    short_store.wait()
    assert len(copies.numbers) == SEMS
    each("drain", *wa, *wb, *back_a.routes, *back_b.routes, back_a, back_b)


def finish(act_in, short_in, full_a, full_b, act_out, short_out, down_out, conv_out, skip_out):
    act_out[...] = act_in[...]
    short_out[...] = short_in[...]

    def rows(full, cut, number, high):
        place = divmod(number, cut.quarter)
        return full[place].astype(F32)[0:high] * (1.0 / 256)

    for tile in range(5):
        lanes = slice(tile * 128, (tile + 1) * 128)
        for row in range(ROW_TILES):
            high = min(SHARD - 16 * row, 16)
            conv_out[16 * row : 16 * row + high, lanes] = rows(full_b, TILES_B, 7 * tile + row, high)
        skip_out[:, lanes] = rows(full_b, TILES_B, 7 * tile + 6, SKIP)
    for tile in range(3):
        wide = min(C0 - tile * 128, 128)
        for row in range(ROW_TILES):
            high = min(SHARD - 16 * row, 16)
            values = rows(full_a, TILES_A, 6 * tile + row, high)
            down_out[16 * row : 16 * row + high, tile * 128 : tile * 128 + wide] = values[:, 0:wide]


def vmem(*shape):
    return pltpu.VMEM(shape, BF)


def tiles(*shape):
    return vmem(*shape, 16, 128)


def body(images, w_down, w_conv, w_skip, act_grad, short_grad):
    picture = images.reshape(512, C0)
    act_cot = act_grad.reshape(CELLS, C1)
    short_cot = short_grad.reshape(CELLS, C1)
    a, b = TILES_A.slots, TILES_B.slots
    slots = []
    for cut in (TILES_A, TILES_B):
        for _, count in cut.routes:
            slots.append(tiles(15, count))
        slots += [tiles(7, cut.quarter), tiles(4, cut.quarter)]

    outs = pl.pallas_call(
        kernel,
        out_shape=(
            jax.ShapeDtypeStruct((CELLS, C1), BF),
            jax.ShapeDtypeStruct((CELLS, C1), BF),
            jax.ShapeDtypeStruct((4, TILES_A.quarter, 16, 128), BF),
            jax.ShapeDtypeStruct((4, TILES_B.quarter, 16, 128), BF),
        ),
        in_specs=[pl.BlockSpec(memory_space=pl.ANY)] * 6,
        out_specs=tuple([pl.BlockSpec(memory_space=pl.ANY)] * 2 + [pl.BlockSpec(memory_space=pltpu.VMEM)] * 2),
        scratch_shapes=[
            vmem(512, C0),
            vmem(SHARD, C0),
            vmem(SHARD, C1),
            vmem(SKIP, C1),
            *[vmem(CELLS, C1)] * 4,
            pltpu.SemaphoreType.DMA((8,)),
            tiles(4, 4, 2, a),
            tiles(4, 4, 2, b),
            tiles(4, 4, 2, a),
            tiles(4, 4, 2, b),
            tiles(4, 4, a),
            tiles(4, 4, b),
            tiles(4, 4, a),
            tiles(4, 4, b),
            vmem(len(PAIRS), LANES0, TILE),
            vmem(512, LANES0),
            vmem(9, CELLS, LANES0),
            vmem(CELLS, COLS),
            vmem(CELLS, COLS),
            vmem(LANES0, LANES0),
            vmem(C1, C1),
            vmem(LANES0, 32 * SKIP_PAD),
            pltpu.SemaphoreType.DMA((SEMS,)),
            *slots,
        ],
        compiler_params=pltpu.CompilerParams(
            collective_id=0, has_side_effects=True, vmem_limit_bytes=56 * 1024 * 1024
        ),
    )(picture, w_down, w_conv, w_skip, act_cot, short_cot)
    activated, shortcut, down, conv, skip = pl.pallas_call(
        finish,
        out_shape=(
            jax.ShapeDtypeStruct((CELLS, C1), BF),
            jax.ShapeDtypeStruct((CELLS, C1), BF),
            jax.ShapeDtypeStruct((SHARD, C0), F32),
            jax.ShapeDtypeStruct((SHARD, C1), F32),
            jax.ShapeDtypeStruct((SKIP, C1), F32),
        ),
        in_specs=[pl.BlockSpec(memory_space=pltpu.VMEM)] * 4,
        out_specs=tuple([pl.BlockSpec(memory_space=pltpu.VMEM)] * 5),
    )(*outs)
    return (
        activated.reshape(act_grad.shape),
        shortcut.reshape(short_grad.shape),
        down,
        conv,
        skip,
    )


def solution(mesh):
    cells = P(("rep", "fsdp"), None, None, None)
    rows = P("fsdp", None)
    return jax.shard_map(
        body,
        mesh=mesh,
        in_specs=(cells, rows, rows, rows, cells, cells),
        out_specs=(cells, cells, rows, rows, rows),
        check_vma=False,
    )
```
